256 devices in a mesh: gx: 4 (over y), gy: 8 (over x, core), gz: 8 (over z).
Axes of the slice: x: 4, y: 4, z: 8, core: 2. Of those that a mesh axis runs over, the one named last changes fastest.
Arguments:
- displacement: float32 [3, 64, 128, 1024], P(None, 'gx', 'gy', 'gz'), may hold values from -0.15 to 0.15
- zone_mass: float32 [64, 128, 1024], P('gx', 'gy', 'gz'), may hold values from 0.5 to 2
- zone_energy: float32 [64, 128, 1024], P('gx', 'gy', 'gz'), may hold values from 0.2 to 5
- slave_position: float32 [65536, 3, 128], P(('gx', 'gy', 'gz')), may hold values from -3 to 3
- slave_stiffness: float32 [65536, 128], P(('gx', 'gy', 'gz')), may hold values from 0.05 to 0.5
- slave_active: int32 [65536, 128], P(('gx', 'gy', 'gz')), may hold values 0 or 1
- partner_peer: int32 [65536, 1], P(('gx', 'gy', 'gz')), may hold values from 0 to 63; in each aligned block of 256 rows (0 to 255, 256 to 511, ...) at most 8 rows name the same one
- partner_block: int32 [65536, 1], P(('gx', 'gy', 'gz')), may hold values from 0 to 63
- master_node: int32 [16384, 128], P(('gx', 'gy', 'gz')), may hold values from 0 to 32767
- master_area: float32 [16384, 3, 128], P(('gx', 'gy', 'gz')), may hold values from -3.6 to 3.6
- face_active: int32 [16384, 128], P(('gx', 'gy', 'gz')), may hold values 0 or 1
Outputs:
- node_force: float32 [3, 64, 128, 1024], P(None, 'gx', 'gy', 'gz')
- slave_force: float32 [65536, 3, 128], P(('gx', 'gy', 'gz'))
The draws below stay inside these ranges and needn't reach their ends.
Inputs may be any that keep to these rules, and one draw needn't show every extreme that they name: `partner_peer`: among the slave blocks of one device, at most 8 name the same partition, and in some devices exactly 8 do. `master_node`: indices repeat freely.
All inputs are finite; a program needn't handle non-finite values. No bound on the sum of `slave_active` or of `face_active` on one device may be relied on, other than what follows from the above.
Results may differ from the reference program's by a relative error of at most 0.000094.
Values sent between devices are 32-bit elements; how exact they have to be, the bound alone decides.
A program may use at most 128 MiB of HBM per device.

```python
import math
import jax
import jax.numpy as jnp
import numpy as np
from jax import lax

CX = 16
CY = 16
CZ = 128
BLOCK = 128
SB = 256
MB = 64
CAP = 8
NX = 64
NY = 128
NZ = 1024
SLAVES = 65536
MASTERS = 16384
N_GY = 8
N_GZ = 8


def place_ends(result, rng, least, largest):
    index_at = [jax.random.randint(jax.random.fold_in(rng, axis), (), 0, length) for axis, length in enumerate(result.shape)]
    widest = result.shape.index(max(result.shape))
    neighbour = index_at[:widest] + [(index_at[widest] + 1) % result.shape[widest]] + index_at[widest + 1:]
    return result.at[tuple(index_at)].set(least).at[tuple(neighbour)].set(largest)


def steps_of(own_key, shape, pieces, smallest, top_value):
    factor_of = 1.0
    for axis_at, shards_of in pieces:
        steps = jax.random.uniform(jax.random.fold_in(jax.random.fold_in(own_key, 6), axis_at), (shards_of,), jnp.float32, smallest / len(pieces), top_value / len(pieces))
        factor_of = factor_of * jnp.repeat(jnp.exp(steps), shape[axis_at] // shards_of).reshape((-1,) + (1,) * (len(shape) - 1 - axis_at))
    return factor_of


def assign_block(stream_key, own, number, rows, count, top, reach, slope):
    order = jax.random.permutation(stream_key, count)
    packed, common = load_shares(count, rows * top, reach, slope, True), load_shares(count, rows * top, reach, slope, False)
    places = jnp.arange(count)

    def named(sizes, offset_by):
        used = int((sizes > 0).sum())
        fixed = max(1, used // 4)
        shifted = fixed + (places - fixed + offset_by * (used - fixed)) % max(1, count - fixed)
        return jnp.zeros((count,), jnp.int32).at[order[jnp.where(places < fixed, places, shifted)]].set(jnp.asarray(sizes, jnp.int32))

    sizes = jnp.where(number % 4 == 0, named(packed, number // 4), named(common, number - number // 4 - 1))
    mixed = jax.random.permutation(jax.random.fold_in(own, 3), count)
    donor, receiver = mixed[0:count // 2 * 2:2], mixed[1:count // 2 * 2:2]
    slack = jnp.minimum(sizes[donor] - 1, reach - sizes[receiver]) // 2
    slack = jnp.where((donor == order[0]) | (receiver == order[0]) | (sizes[receiver] == 0), 0, jnp.maximum(slack, 0))
    shifted = jax.random.randint(jax.random.fold_in(own, 4), (count // 2,), 0, 1 << 20) % (slack + 1)
    sizes = sizes.at[donor].add(-shifted).at[receiver].add(shifted)
    labels = jnp.searchsorted(jnp.cumsum(sizes), jnp.arange(rows * top), side="right").astype(jnp.int32)
    table = labels.reshape(top, rows).T
    table = table[jax.random.permutation(jax.random.fold_in(own, 1), rows)]
    offset_by = jax.random.randint(jax.random.fold_in(own, 2), (rows, 1), 0, top)
    return jnp.take_along_axis(table, (jnp.arange(top)[None, :] + offset_by) % top, axis=1)


def load_shares(count, total, bound, slope, full):
    loads = [(1 << 20) // math.isqrt(rank ** slope) + 1 for rank in range(1, count + 1)]
    largest = bound if full else min(bound, max(-(-total // count), total * loads[0] // sum(loads)))
    least = 1 if total - largest >= count - 1 else 0
    counts, rest = [largest] + [least] * (count - 1), total - largest - least * (count - 1)
    while rest > 0:
        candidates = [i for i in range(1, count) if counts[i] < largest] or [i for i in range(1, count) if counts[i] < bound]
        whole, budget = sum([loads[i] for i in candidates]), rest
        for i in candidates:
            extra = min(bound - counts[i], max(1, budget * loads[i] // whole), rest)
            counts[i] = counts[i] + extra
            rest = rest - extra
    return np.array(counts)


def noise(own_key, extent, width, limit, pieces=(), kind=jnp.bfloat16):
    entries = jax.random.normal(own_key, extent, jnp.float32) * width
    if len(pieces) > 0:
        entries = steps_of(own_key, extent, pieces, -0.22, 0.18) * entries
    return jnp.clip(entries, min=-limit, max=limit).astype(kind)


def setup_inputs(seed: int = 0) -> dict:
    streams_of = jax.random.split(jax.random.key(seed), 12)
    displacement = jnp.clip(jax.random.uniform(streams_of[0], (3, NX, NY, NZ), jnp.float32, -0.15, 0.15) * steps_of(streams_of[0], (3, NX, NY, NZ), ((1, 4), (2, 8), (3, 8)), -0.4, 0.0), -0.15, 0.15)
    zone_mass = jnp.clip(jnp.exp(math.log(2.0) - 1.3862944 * jax.random.uniform(streams_of[1], (NX, NY, NZ), jnp.float32) ** steps_of(streams_of[1], (NX, NY, NZ), ((0, 4), (1, 8), (2, 8)), -0.2, 0.2)), 0.5, 2.0)
    zone_energy = jnp.clip(jnp.exp(math.log(5.0) - 3.218876 * jax.random.uniform(streams_of[2], (NX, NY, NZ), jnp.float32) ** steps_of(streams_of[2], (NX, NY, NZ), ((0, 4), (1, 8), (2, 8)), -0.2, 0.2)), 0.2, 5.0)
    slave_position = noise(streams_of[3], (SLAVES, 3, BLOCK), 0.5, 3.0, ((0, 256),), jnp.float32)
    slave_stiffness = jnp.clip(jnp.exp(math.log(0.5) - 2.3025851 * jax.random.uniform(streams_of[4], (SLAVES, BLOCK), jnp.float32) ** steps_of(streams_of[4], (SLAVES, BLOCK), ((0, 256),), -0.2, 0.2)), 0.05, 0.5)
    slave_active = place_ends((jax.random.randint(streams_of[5], (SLAVES, BLOCK), 0, 4) < 3).astype(jnp.int32), jax.random.fold_in(streams_of[5], 1), 0, 1)
    partner_peer_keys = jax.random.split(jax.random.fold_in(streams_of[6], 1), SLAVES // SB)
    partner_peer_turns = jax.random.permutation(jax.random.fold_in(streams_of[6], 3), SLAVES // SB)
    partner_peer = jax.vmap(lambda own, number: assign_block(jax.random.fold_in(streams_of[6], 2), own, number, SB, N_GY * N_GZ, 1, CAP, 2))(partner_peer_keys, partner_peer_turns).reshape((SLAVES, 1))
    partner_block = place_ends(jax.random.randint(streams_of[7], (SLAVES, 1), 0, MB), jax.random.fold_in(streams_of[7], 1), 0, MB - 1).astype(jnp.int32)
    master_node = place_ends(jax.random.randint(streams_of[8], (MASTERS, BLOCK), 0, CX * CY * CZ), jax.random.fold_in(streams_of[8], 1), 0, (CX * CY * CZ) - 1).astype(jnp.int32)
    master_area = noise(streams_of[9], (MASTERS, 3, BLOCK), 0.6, 3.6, ((0, 256),), jnp.float32)
    face_active = place_ends((jax.random.randint(streams_of[10], (MASTERS, BLOCK), 0, 4) < 3).astype(jnp.int32), jax.random.fold_in(streams_of[10], 1), 0, 1)
    return {"displacement": displacement, "zone_mass": zone_mass, "zone_energy": zone_energy, "slave_position": slave_position, "slave_stiffness": slave_stiffness, "slave_active": slave_active, "partner_peer": partner_peer, "partner_block": partner_block, "master_node": master_node, "master_area": master_area, "face_active": face_active}


gamma_gas = 5.0 / 3.0
corner_offsets = [(0, 0, 0), (0, 0, 1), (0, 1, 0), (0, 1, 1), (1, 0, 0), (1, 0, 1), (1, 1, 0), (1, 1, 1)]


def cross_parts(left, right):
    return [left[1] * right[2] - left[2] * right[1],
            left[2] * right[0] - left[0] * right[2],
            left[0] * right[1] - left[1] * right[0]]


def zone_state(corner_moves, masses, energies, valid):
    edges = []
    for axis_pick in range(3):
        parts = []
        for comp in range(3):
            total = jnp.zeros_like(masses)
            for moved, offset in zip(corner_moves, corner_offsets):
                total = total + (2.0 * offset[axis_pick] - 1.0) * moved[comp]
            total = total * 0.25
            if comp == axis_pick:
                total = total + 1.0
            parts.append(total)
        edges.append(parts)
    cross_yz = cross_parts(edges[1], edges[2])
    cross_zx = cross_parts(edges[2], edges[0])
    cross_xy = cross_parts(edges[0], edges[1])
    volume = edges[0][0] * cross_yz[0] + edges[0][1] * cross_yz[1] + edges[0][2] * cross_yz[2]
    pressure = jnp.where(valid, (gamma_gas - 1.0) * masses * energies / jnp.where(valid, volume, 1.0), 0.0)
    return pressure, cross_yz, cross_zx, cross_xy


def corner_force(state, offset):
    pressure, cross_yz, cross_zx, cross_xy = state
    sign_x = 2.0 * offset[0] - 1.0
    sign_y = 2.0 * offset[1] - 1.0
    sign_z = 2.0 * offset[2] - 1.0
    return jnp.stack([pressure * 0.25 * (sign_x * cross_yz[comp] + sign_y * cross_zx[comp] + sign_z * cross_xy[comp]) for comp in range(3)])


def contact_block(position, stiffness, centers, areas, active):
    center_dot = centers[0] * areas[0] + centers[1] * areas[1] + centers[2] * areas[2]
    signed_gap = (position[0][:, None] * areas[0][None, :] + position[1][:, None] * areas[1][None, :]
                  + position[2][:, None] * areas[2][None, :] - center_dot[None, :])
    intersection = jnp.maximum(-signed_gap, 0.0) * active[None, :]
    slave_push = stiffness[None, :] * jnp.dot(areas, intersection.T, precision=lax.Precision.HIGHEST)
    face_push = -areas * jnp.dot(stiffness, intersection, precision=lax.Precision.HIGHEST)[None, :]
    return slave_push, face_push


def reference(displacement, zone_mass, zone_energy, slave_position, slave_stiffness, slave_active, partner_peer, partner_block, master_node, master_area, face_active):
    shape3 = (NX, NY, NZ)
    valid = ((lax.broadcasted_iota(jnp.int32, shape3, 0) < NX - 1)
             & (lax.broadcasted_iota(jnp.int32, shape3, 1) < NY - 1)
             & (lax.broadcasted_iota(jnp.int32, shape3, 2) < NZ - 1))
    padded_up = jnp.pad(displacement, ((0, 0), (0, 1), (0, 1), (0, 1)))
    corner_moves = [padded_up[:, a:a + NX, b:b + NY, e:e + NZ] for (a, b, e) in corner_offsets]
    state = zone_state(corner_moves, zone_mass, zone_energy, valid)
    node_force = jnp.zeros((3, NX, NY, NZ), jnp.float32)
    for offset in corner_offsets:
        a, b, e = offset
        padded_low = jnp.pad(corner_force(state, offset), ((0, 0), (1, 0), (1, 0), (1, 0)))
        node_force = node_force + padded_low[:, 1 - a:1 - a + NX, 1 - b:1 - b + NY, 1 - e:1 - e + NZ]

    peers = N_GY * N_GZ
    master_ids = jnp.arange(MASTERS, dtype=jnp.int32)
    owner = master_ids // MB
    owner_x = owner // peers
    owner_y = (owner // N_GZ) % N_GY
    owner_z = owner % N_GZ
    local_flat = master_node
    local_i = local_flat // (CY * CZ)
    local_j = (local_flat // CZ) % CY
    local_k = local_flat % CZ
    global_flat = (((owner_x[:, None] * CX + local_i) * NY + owner_y[:, None] * CY + local_j) * NZ
                   + owner_z[:, None] * CZ + local_k).astype(jnp.int32)
    flat_moves = displacement.reshape(3, -1)
    centers = jnp.transpose(flat_moves[:, global_flat], (1, 0, 2))
    face_live = face_active.astype(jnp.float32)

    slave_owner = jnp.arange(SLAVES, dtype=jnp.int32) // SB
    paired = ((slave_owner // peers) * peers + partner_peer[:, 0]) * MB + partner_block[:, 0]
    stiffness = slave_stiffness * slave_active.astype(jnp.float32)

    def per_block(items):
        position, stiff_row, pair_id = items
        return contact_block(position, stiff_row, centers[pair_id], master_area[pair_id], face_live[pair_id])

    slave_force, face_terms = lax.map(per_block, (slave_position, stiffness, paired.astype(jnp.int32)))
    reactions = jax.ops.segment_sum(face_terms, paired, num_segments=MASTERS)
    reaction_flat = jnp.transpose(reactions, (1, 0, 2)).reshape(3, -1)
    total_flat = node_force.reshape(3, -1).at[:, global_flat.reshape(-1)].add(reaction_flat)
    return total_flat.reshape(3, NX, NY, NZ), slave_force
```

```python
import functools

import jax
import jax.numpy as jnp
from jax import lax
from jax.experimental import pallas as pl
from jax.experimental.pallas import tpu as pltpu
from jax.sharding import PartitionSpec as P

f32 = jnp.float32
bf16 = jnp.bfloat16
i32 = jnp.int32
NT = (((1,), (1,)), ((), ()))
MESH = pl.DeviceIdType.MESH
VMEM = pl.BlockSpec(memory_space=pltpu.VMEM)
SLOTS = 8
LANES = 128

gamma_gas = 5.0 / 3.0
corner_offsets = [
    (0, 0, 0),
    (0, 0, 1),
    (0, 1, 0),
    (0, 1, 1),
    (1, 0, 0),
    (1, 0, 1),
    (1, 1, 0),
    (1, 1, 1),
]


def split3(x):
    first = x.astype(bf16)
    rest = x - first.astype(f32)
    second = rest.astype(bf16)
    third = (rest - second.astype(f32)).astype(bf16)
    return first, second, third


def dot(left, right):
    return jnp.dot(left, right, preferred_element_type=f32)


def iota(shape, axis):
    return lax.broadcasted_iota(i32, shape, axis)


def gather_centers(disp, mnode, centers, table):
    rows = disp.shape[1] * disp.shape[2]
    for c in range(3):
        turned = jnp.transpose(disp[c].reshape(rows, LANES))
        for s, part in enumerate(split3(turned)):
            table[c * LANES : (c + 1) * LANES, s * rows : (s + 1) * rows] = part
    row_at = iota((rows, 2 * LANES), 0)
    lane_at = iota((LANES, 2 * LANES), 0)

    def step(q, carry):
        index = jnp.concatenate([mnode[pl.ds(2 * q + u, 1), :] for u in range(2)], axis=1)
        hot = (lax.shift_right_logical(index, 7) == row_at).astype(f32).astype(bf16)
        picked = dot(table[...], jnp.concatenate([hot, hot, hot], axis=0))
        here = (index & (LANES - 1)) == lane_at
        for c in range(3):
            row = jnp.sum(
                jnp.where(here, picked[c * LANES : (c + 1) * LANES], 0.0), axis=0, keepdims=True
            )
            for u in range(2):
                centers[c, pl.ds(2 * q + u, 1), :] = row[:, u * LANES : (u + 1) * LANES]
        return carry

    lax.fori_loop(0, mnode.shape[0] // 2, step, 0, unroll=4)


def contact_slots(master, slave):
    m1, m2, m3 = [part.astype(f32) for part in split3(master)]
    s1, s2, s3 = [part.astype(f32) for part in split3(slave)]
    zero = jnp.zeros_like(master)
    turned = jnp.concatenate(
        [
            jnp.transpose(jnp.concatenate([m1, m2, m3, m1], axis=0)),
            jnp.transpose(jnp.concatenate([m2, m1, zero, zero], axis=0)),
        ],
        axis=1,
    ).astype(bf16)
    weights = jnp.concatenate([s1, s1, s1, s2, s2, s3, zero, zero], axis=0)
    slot_row = iota((256, LANES), 0) & (SLOTS - 1)
    areas = jnp.concatenate([m1[:24], zero[:8], m2[:24], zero[:8]], axis=0).astype(bf16)
    areas = jnp.concatenate([areas, areas], axis=1)
    push_row = iota((64, LANES), 0) & (SLOTS - 1)
    push = jnp.zeros((64, LANES), f32)
    columns = []
    for q in range(SLOTS // 2):
        chosen = jnp.concatenate(
            [jnp.where(slot_row == 2 * q + u, weights, 0.0).astype(bf16) for u in range(2)], axis=1
        )
        depth = jnp.maximum(dot(turned, chosen), 0.0)
        high = depth.astype(bf16)
        low = (depth - high.astype(f32)).astype(bf16)
        sums = dot(areas, jnp.concatenate([high, low], axis=0))
        for u in range(2):
            half = slice(u * LANES, (u + 1) * LANES)
            push = jnp.where(push_row == 2 * q + u, sums[:, half], push)
            columns.append(jnp.sum(depth[:, half], axis=1, keepdims=True))
    return push[:24] + push[32:56], jnp.transpose(jnp.concatenate(columns, axis=1))


def exchange_kernel(
    size_y,
    size_z,
    disp,
    spos,
    sstiff,
    sactive,
    peer,
    block,
    mnode,
    marea,
    factive,
    push_out,
    total_out,
    place_out,
    ask_send,
    ask_recv,
    give_send,
    give_recv,
    back_send,
    back_recv,
    slave,
    centers,
    table,
    hot_t,
    ask_sems,
    give_sems,
    back_sems,
):
    peers = size_y * size_z
    count = peer.shape[1]
    masters = mnode.shape[0]
    gx, gy, gz = lax.axis_index("gx"), lax.axis_index("gy"), lax.axis_index("gz")

    def device_ahead(t):
        return (gx, lax.rem(gy + t // size_z, size_y), lax.rem(gz + t % size_z, size_z))

    def device_behind(t):
        return (
            gx,
            lax.rem(gy + size_y - t // size_z, size_y),
            lax.rem(gz + size_z - t % size_z, size_z),
        )

    barrier = pltpu.get_barrier_semaphore()

    def greet(t, carry):
        pl.semaphore_signal(barrier, inc=1, device_id=device_ahead(t), device_id_type=MESH)
        return carry

    lax.fori_loop(1, peers, greet, 0)

    named = peer[...]
    ahead = lax.rem(named // size_z - gy + size_y, size_y) * size_z + lax.rem(
        named % size_z - gz + size_z, size_z
    )
    to_peer = (ahead == iota((peers, count), 0)).astype(f32)
    before = (iota((count, count), 0) < iota((count, count), 1)).astype(f32).astype(bf16)
    rank = jnp.sum(to_peer * dot(to_peer.astype(bf16), before), axis=0, keepdims=True).astype(i32)
    place = ahead * SLOTS + rank
    place_out[...] = jnp.broadcast_to(place, place_out.shape)
    in_rank = jnp.where(rank == iota((LANES, count), 0), (block[...] + 1).astype(f32), 0.0)
    asked = lax.dot_general(
        to_peer.astype(bf16), in_rank.astype(bf16), NT, preferred_element_type=f32
    )
    for t in range(peers):
        ask_send[t] = asked[t : t + 1, :]
    ask_recv[0] = asked[0:1, :]

    pl.semaphore_wait(barrier, peers - 1)

    def ask_copy(t):
        return pltpu.make_async_remote_copy(
            src_ref=ask_send.at[t],
            dst_ref=ask_recv.at[t],
            send_sem=ask_sems.at[0, t],
            recv_sem=ask_sems.at[1, t],
            device_id=device_ahead(t),
            device_id_type=MESH,
        )

    def give_copy(t):
        return pltpu.make_async_remote_copy(
            src_ref=give_send.at[t],
            dst_ref=give_recv.at[t],
            send_sem=give_sems.at[0, t],
            recv_sem=give_sems.at[1, t],
            device_id=device_behind(t),
            device_id_type=MESH,
        )

    def back_copy(t):
        return pltpu.make_async_remote_copy(
            src_ref=back_send.at[t],
            dst_ref=back_recv.at[t],
            send_sem=back_sems.at[0, t],
            recv_sem=back_sems.at[1, t],
            device_id=device_ahead(t),
            device_id_type=MESH,
        )

    def ask_start(t, carry):
        ask_copy(t).start()
        return carry

    lax.fori_loop(1, peers, ask_start, 0)

    gather_centers(disp, mnode, centers, table)
    live = factive[...].astype(f32)
    areas = [marea[c] * live for c in range(3)]
    moved = areas[0] * centers[0] + areas[1] * centers[1] + areas[2] * centers[2]
    pack = jnp.concatenate(areas + [moved], axis=1)
    pack3 = jnp.concatenate(split3(pack), axis=0)

    def ask_wait(t, carry):
        ask_copy(t).wait_recv()
        return carry

    lax.fori_loop(1, peers, ask_wait, 0)
    diagonal = (iota((peers, SLOTS, LANES), 1) == iota((peers, SLOTS, LANES), 2)).astype(f32)
    wanted = jnp.sum(
        jnp.broadcast_to(ask_recv[...], (peers, SLOTS, LANES)) * diagonal, axis=2, keepdims=True
    )
    wanted = wanted.astype(i32).reshape(peers * SLOTS, 1) - 1
    hot = (wanted == iota((peers * SLOTS, masters), 1)).astype(f32)
    hot_t[...] = jnp.transpose(
        (wanted == iota((peers * SLOTS, LANES), 1)).astype(f32)
    ).astype(bf16)
    hot3 = jnp.concatenate([hot, hot, hot], axis=1).astype(bf16)
    given = dot(hot3, pack3)
    for c in range(4):
        give_send[:, c * SLOTS : (c + 1) * SLOTS, :] = given[
            :, c * LANES : (c + 1) * LANES
        ].reshape(peers, SLOTS, LANES)

    def give_start(t, carry):
        give_copy(t).start()
        return carry

    lax.fori_loop(1, peers, give_start, 0)
    give_recv[0] = give_send[0]

    stiff = sstiff[...] * sactive[...].astype(f32)
    slots = (place == iota((peers * SLOTS, count), 0)).astype(f32).astype(bf16)
    for c in range(4):
        field = stiff if c == 3 else -(stiff * spos[c])
        parts = split3(field)
        rows = dot(slots, parts[0]) + dot(slots, parts[1]) + dot(slots, parts[2])
        slave[:, c * SLOTS : (c + 1) * SLOTS, :] = rows.reshape(peers, SLOTS, LANES)

    step_of = 4

    def contact(q, carry):
        for u in range(step_of):
            t = q * step_of + u

            @pl.when(t > 0)
            def _():
                give_copy(t).wait_recv()

        for u in range(step_of):
            t = q * step_of + u
            push, total = contact_slots(give_recv[t], slave[t])
            push_out[t] = push
            back_send[t] = total
        for u in range(step_of):
            t = q * step_of + u

            @pl.when(t > 0)
            def _():
                back_copy(t).start()

        return carry

    lax.fori_loop(0, peers // step_of, contact, 0)
    back_recv[0] = back_send[0]

    def finish(t, carry):
        back_copy(t).wait_recv()
        back_copy(t).wait_send()
        give_copy(t).wait_send()
        ask_copy(t).wait_send()
        return carry

    lax.fori_loop(1, peers, finish, 0)
    parts = split3(back_recv[...].reshape(peers * SLOTS, LANES))
    turned = hot_t[0:masters, :]
    total_out[...] = dot(turned, parts[0]) + dot(turned, parts[1]) + dot(turned, parts[2])


def scatter_kernel(push, total, place, mnode, marea, zone, node_out, slave_out, grid):
    masters = mnode.shape[0]
    peers = push.shape[0]
    count = place.shape[1]
    rows = zone.shape[1]

    turned = jnp.transpose(place[...])
    slots = (turned[:, 0:1] == iota((count, peers * SLOTS), 1)).astype(f32).astype(bf16)
    for c in range(3):
        field = push[:, c * SLOTS : (c + 1) * SLOTS, :].reshape(peers * SLOTS, LANES)
        parts = split3(field)
        slave_out[c] = dot(slots, parts[0]) + dot(slots, parts[1]) + dot(slots, parts[2])

    row_at = iota((rows, 2 * LANES), 0)
    lane_at = iota((LANES, 2 * LANES), 0)
    grid[...] = jnp.zeros_like(grid)

    def step(q, carry):
        pair = [pl.ds(2 * q + u, 1) for u in range(2)]
        index = jnp.concatenate([mnode[at, :] for at in pair], axis=1)
        hot = (lax.shift_right_logical(index, 7) == row_at).astype(f32).astype(bf16)
        here = (index & (LANES - 1)) == lane_at
        high, low = [], []
        for c in range(3):
            force = -jnp.concatenate([marea[c, at, :] * total[at, :] for at in pair], axis=1)
            first = force.astype(bf16).astype(f32)
            high.append(jnp.where(here, first, 0.0).astype(bf16))
            low.append(jnp.where(here, force - first, 0.0).astype(bf16))
        spread = jnp.concatenate(
            [jnp.concatenate(high, axis=0), jnp.concatenate(low, axis=0)], axis=1
        )
        grid[...] += lax.dot_general(
            spread, jnp.concatenate([hot, hot], axis=1), NT, preferred_element_type=f32
        )
        return carry

    lax.fori_loop(0, masters // 2, step, 0, unroll=4)
    for c in range(3):
        node_out[c] = zone[c] + jnp.transpose(grid[c * LANES : (c + 1) * LANES, :])


def extended_2(cells, sides, width):
    for axis, dim in sides:
        count = lax.axis_size(axis)
        ends = count - 1
        head = lax.slice_in_dim(cells, 0, width, axis=dim)
        tail = lax.slice_in_dim(cells, cells.shape[dim] - width, cells.shape[dim], axis=dim)
        cells = jnp.concatenate(
            [
                lax.ppermute(tail, axis, [(i, (i + 1) % count) for i in range(ends)]),
                cells,
                lax.ppermute(head, axis, [((i + 1) % count, i) for i in range(ends)]),
            ],
            axis=dim,
        )
    return cells


def cross_parts(left, right):
    return [
        left[1] * right[2] - left[2] * right[1],
        left[2] * right[0] - left[0] * right[2],
        left[0] * right[1] - left[1] * right[0],
    ]


def zone_state(corner_moves, masses, energies, valid):
    edges = []
    for axis_pick in range(3):
        parts = []
        for comp in range(3):
            total = jnp.zeros_like(masses)
            for moved, offset in zip(corner_moves, corner_offsets):
                total = total + (2.0 * offset[axis_pick] - 1.0) * moved[comp]
            total = total * 0.25
            if comp == axis_pick:
                total = total + 1.0
            parts.append(total)
        edges.append(parts)
    cross_yz = cross_parts(edges[1], edges[2])
    cross_zx = cross_parts(edges[2], edges[0])
    cross_xy = cross_parts(edges[0], edges[1])
    volume = edges[0][0] * cross_yz[0] + edges[0][1] * cross_yz[1] + edges[0][2] * cross_yz[2]
    pressure = jnp.where(
        valid, (gamma_gas - 1.0) * masses * energies / jnp.where(valid, volume, 1.0), 0.0
    )
    return (pressure, cross_yz, cross_zx, cross_xy)


def corner_force(state, offset):
    pressure, cross_yz, cross_zx, cross_xy = state
    sign_x = 2.0 * offset[0] - 1.0
    sign_y = 2.0 * offset[1] - 1.0
    sign_z = 2.0 * offset[2] - 1.0
    return jnp.stack(
        [
            pressure
            * 0.25
            * (sign_x * cross_yz[comp] + sign_y * cross_zx[comp] + sign_z * cross_xy[comp])
            for comp in range(3)
        ]
    )


def axis_valid(position, count, length):
    global_row = position * count + jnp.arange(count + 1, dtype=jnp.int32) - 1
    return (global_row >= 0) & (global_row <= length - 2)


def zone_part(displacement, zone_mass, zone_energy):
    cells_x, cells_y, cells_z = (
        displacement.shape[1],
        displacement.shape[2],
        displacement.shape[3],
    )
    fields = jnp.concatenate([displacement, zone_mass[None], zone_energy[None]], axis=0)
    extended = extended_2(fields, (("gx", 1), ("gy", 2), ("gz", 3)), 1)
    valid_x = axis_valid(lax.axis_index("gx"), cells_x, cells_x * lax.axis_size("gx"))
    valid_y = axis_valid(lax.axis_index("gy"), cells_y, cells_y * lax.axis_size("gy"))
    valid_z = axis_valid(lax.axis_index("gz"), cells_z, cells_z * lax.axis_size("gz"))
    valid = valid_x[:, None, None] & valid_y[None, :, None] & valid_z[None, None, :]
    corner_moves = [
        extended[0:3, a : a + cells_x + 1, b : b + cells_y + 1, e : e + cells_z + 1]
        for a, b, e in corner_offsets
    ]
    masses = extended[3, : cells_x + 1, : cells_y + 1, : cells_z + 1]
    energies = extended[4, : cells_x + 1, : cells_y + 1, : cells_z + 1]
    state = zone_state(corner_moves, masses, energies, valid)
    node_force = jnp.zeros((3, cells_x, cells_y, cells_z), jnp.float32)
    for offset in corner_offsets:
        a, b, e = offset
        forces = corner_force(state, offset)
        node_force = (
            node_force
            + forces[:, 1 - a : 1 - a + cells_x, 1 - b : 1 - b + cells_y, 1 - e : 1 - e + cells_z]
        )
    return node_force


def body(
    displacement,
    zone_mass,
    zone_energy,
    slave_position,
    slave_stiffness,
    slave_active,
    partner_peer,
    partner_block,
    master_node,
    master_area,
    face_active,
):
    size_y = lax.axis_size("gy")
    size_z = lax.axis_size("gz")
    peers = size_y * size_z
    count = slave_position.shape[0]
    masters = master_node.shape[0]
    cells = displacement.shape[1:]
    rows = cells[0] * cells[1]
    area = jnp.transpose(master_area, (1, 0, 2))
    push, total, place = pl.pallas_call(
        functools.partial(exchange_kernel, size_y, size_z),
        out_shape=(
            jax.ShapeDtypeStruct((peers, 24, LANES), f32),
            jax.ShapeDtypeStruct((masters, LANES), f32),
            jax.ShapeDtypeStruct((8, count), i32),
        ),
        in_specs=[VMEM] * 9,
        out_specs=(VMEM,) * 3,
        scratch_shapes=[
            pltpu.VMEM((peers, 1, LANES), f32),
            pltpu.VMEM((peers, 1, LANES), f32),
            pltpu.VMEM((peers, 32, LANES), f32),
            pltpu.VMEM((peers, 32, LANES), f32),
            pltpu.VMEM((peers, 8, LANES), f32),
            pltpu.VMEM((peers, 8, LANES), f32),
            pltpu.VMEM((peers, 32, LANES), f32),
            pltpu.VMEM((3, masters, LANES), f32),
            pltpu.VMEM((3 * LANES, 3 * rows), bf16),
            pltpu.VMEM((LANES, peers * SLOTS), bf16),
            pltpu.SemaphoreType.DMA((2, peers)),
            pltpu.SemaphoreType.DMA((2, peers)),
            pltpu.SemaphoreType.DMA((2, peers)),
        ],
        compiler_params=pltpu.CompilerParams(
            collective_id=0, has_side_effects=True, vmem_limit_bytes=48 * 2**20
        ),
        name="exchange",
    )(
        displacement,
        jnp.transpose(slave_position, (1, 0, 2)),
        slave_stiffness,
        slave_active,
        partner_peer.reshape(1, count),
        partner_block.reshape(1, count),
        master_node,
        area,
        face_active,
    )
    zone = zone_part(displacement, zone_mass, zone_energy)
    node_force, slave_force = pl.pallas_call(
        scatter_kernel,
        out_shape=(
            jax.ShapeDtypeStruct((3, rows, LANES), f32),
            jax.ShapeDtypeStruct((3, count, LANES), f32),
        ),
        in_specs=[VMEM] * 6,
        out_specs=(VMEM,) * 2,
        scratch_shapes=[pltpu.VMEM((3 * LANES, rows), f32)],
        compiler_params=pltpu.CompilerParams(vmem_limit_bytes=48 * 2**20),
        name="scatter",
    )(push, total, place, master_node, area, zone.reshape(3, rows, LANES))
    return (
        node_force.reshape((3,) + cells),
        jnp.transpose(slave_force, (1, 0, 2)),
    )


def solution(mesh):
    return jax.shard_map(
        body,
        mesh=mesh,
        in_specs=(
            P(None, "gx", "gy", "gz"),
            P("gx", "gy", "gz"),
            P("gx", "gy", "gz"),
            P(("gx", "gy", "gz"), None, None),
            P(("gx", "gy", "gz"), None),
            P(("gx", "gy", "gz"), None),
            P(("gx", "gy", "gz"), None),
            P(("gx", "gy", "gz"), None),
            P(("gx", "gy", "gz"), None),
            P(("gx", "gy", "gz"), None, None),
            P(("gx", "gy", "gz"), None),
        ),
        out_specs=(P(None, "gx", "gy", "gz"), P(("gx", "gy", "gz"), None, None)),
        check_vma=False,
    )
```

```python
import functools

import jax
import jax.numpy as jnp
from jax import lax
from jax.experimental import pallas as pl
from jax.experimental.pallas import tpu as pltpu
from jax.sharding import PartitionSpec as P

f32 = jnp.float32
bf16 = jnp.bfloat16
i32 = jnp.int32
NT = (((1,), (1,)), ((), ()))
MESH = pl.DeviceIdType.MESH
VMEM = pl.BlockSpec(memory_space=pltpu.VMEM)
SLOTS = 8
LANES = 128

gamma_gas = 5.0 / 3.0


def split3(x):
    first = x.astype(bf16)
    rest = x - first.astype(f32)
    second = rest.astype(bf16)
    third = (rest - second.astype(f32)).astype(bf16)
    return first, second, third


def dot(left, right):
    return jnp.dot(left, right, preferred_element_type=f32)


def iota(shape, axis):
    return lax.broadcasted_iota(i32, shape, axis)


def gather_centers(disp, mnode, centers, table):
    rows = disp.shape[1] * disp.shape[2]
    for c in range(3):
        turned = jnp.transpose(disp[c].reshape(rows, LANES))
        for s, part in enumerate(split3(turned)):
            table[c * LANES : (c + 1) * LANES, s * rows : (s + 1) * rows] = part
    row_at = iota((rows, 2 * LANES), 0)
    lane_at = iota((LANES, 2 * LANES), 0)

    def step(q, carry):
        index = jnp.concatenate([mnode[pl.ds(2 * q + u, 1), :] for u in range(2)], axis=1)
        hot = (lax.shift_right_logical(index, 7) == row_at).astype(f32).astype(bf16)
        picked = dot(table[...], jnp.concatenate([hot, hot, hot], axis=0))
        here = (index & (LANES - 1)) == lane_at
        for c in range(3):
            row = jnp.sum(
                jnp.where(here, picked[c * LANES : (c + 1) * LANES], 0.0), axis=0, keepdims=True
            )
            for u in range(2):
                centers[c, pl.ds(2 * q + u, 1), :] = row[:, u * LANES : (u + 1) * LANES]
        return carry

    lax.fori_loop(0, mnode.shape[0] // 2, step, 0, unroll=4)


def contact_slots(master, slave):
    m1, m2, m3 = [part.astype(f32) for part in split3(master)]
    s1, s2, s3 = [part.astype(f32) for part in split3(slave)]
    zero = jnp.zeros_like(master)
    turned = jnp.concatenate(
        [
            jnp.transpose(jnp.concatenate([m1, m2, m3, m1], axis=0)),
            jnp.transpose(jnp.concatenate([m2, m1, zero, zero], axis=0)),
        ],
        axis=1,
    ).astype(bf16)
    weights = jnp.concatenate([s1, s1, s1, s2, s2, s3, zero, zero], axis=0)
    slot_row = iota((256, LANES), 0) & (SLOTS - 1)
    areas = jnp.concatenate([m1[:24], zero[:8], m2[:24], zero[:8]], axis=0).astype(bf16)
    areas = jnp.concatenate([areas, areas], axis=1)
    push_row = iota((64, LANES), 0) & (SLOTS - 1)
    push = jnp.zeros((64, LANES), f32)
    columns = []
    for q in range(SLOTS // 2):
        chosen = jnp.concatenate(
            [jnp.where(slot_row == 2 * q + u, weights, 0.0).astype(bf16) for u in range(2)], axis=1
        )
        depth = jnp.maximum(dot(turned, chosen), 0.0)
        high = depth.astype(bf16)
        low = (depth - high.astype(f32)).astype(bf16)
        sums = dot(areas, jnp.concatenate([high, low], axis=0))
        for u in range(2):
            half = slice(u * LANES, (u + 1) * LANES)
            push = jnp.where(push_row == 2 * q + u, sums[:, half], push)
            columns.append(jnp.sum(depth[:, half], axis=1, keepdims=True))
    return push[:24] + push[32:56], jnp.transpose(jnp.concatenate(columns, axis=1))


def cross_parts(left, right):
    return [
        left[1] * right[2] - left[2] * right[1],
        left[2] * right[0] - left[0] * right[2],
        left[0] * right[1] - left[1] * right[0],
    ]


def z_and_y_sums(near, far, rows):
    total, change = near + far, far - near
    total_up = pltpu.roll(total, rows - 1, 0)
    change_up = pltpu.roll(change, rows - 1, 0)
    return total + total_up, total_up - total, change + change_up


def zone_terms(low, high, mass, energy, valid):
    edge_x = [0.25 * (high[c][0] - low[c][0]) + (1.0 if c == 0 else 0.0) for c in range(3)]
    edge_y = [0.25 * (low[c][1] + high[c][1]) + (1.0 if c == 1 else 0.0) for c in range(3)]
    edge_z = [0.25 * (low[c][2] + high[c][2]) + (1.0 if c == 2 else 0.0) for c in range(3)]
    across_yz = cross_parts(edge_y, edge_z)
    across_zx = cross_parts(edge_z, edge_x)
    across_xy = cross_parts(edge_x, edge_y)
    volume = edge_x[0] * across_yz[0] + edge_x[1] * across_yz[1] + edge_x[2] * across_yz[2]
    pressure = jnp.where(
        valid, (gamma_gas - 1.0) * mass * energy / jnp.where(valid, volume, 1.0), 0.0
    )
    quarter = 0.25 * pressure
    return [[quarter * part for part in parts] for parts in (across_yz, across_zx, across_xy)]


class Halo:
    def __init__(self, disp, mass, energy, held, y_send, y_recv, z_send, z_recv, sems, sizes):
        self.disp, self.mass, self.energy, self.held = disp, mass, energy, held
        self.y_send, self.y_recv, self.z_send, self.z_recv = y_send, y_recv, z_send, z_recv
        self.sems, self.sizes = sems, sizes
        self.at = [lax.axis_index(axis) for axis in ("gx", "gy", "gz")]
        self.cells_x, self.cells_y = disp.shape[1], disp.shape[2]
        self.rows = held.shape[2]

    def beside(self, axis, shift):
        place = list(self.at)
        place[axis] = lax.rem(place[axis] + self.sizes[axis] + shift, self.sizes[axis])
        return tuple(place)

    def copy(self, number, source, target, axis, shift):
        return pltpu.make_async_remote_copy(
            src_ref=source,
            dst_ref=target,
            send_sem=self.sems.at[0, number],
            recv_sem=self.sems.at[1, number],
            device_id=self.beside(axis, shift),
            device_id_type=MESH,
        )

    def x_copies(self):
        last, own = self.cells_x - 1, pl.ds(0, self.cells_y)
        return [
            self.copy(0, self.disp.at[:, last], self.held.at[pl.ds(0, 3), 0, own], 0, 1),
            self.copy(1, self.mass.at[last], self.held.at[3, 0, own], 0, 1),
            self.copy(2, self.energy.at[last], self.held.at[4, 0, own], 0, 1),
            self.copy(3, self.disp.at[:, 0], self.held.at[pl.ds(0, 3), last + 2, own], 0, -1),
        ]

    def y_copies(self):
        return [
            self.copy(4, self.y_send.at[pl.ds(0, 5)], self.y_recv.at[pl.ds(0, 5)], 1, 1),
            self.copy(5, self.y_send.at[pl.ds(5, 3)], self.y_recv.at[pl.ds(5, 3)], 1, -1),
        ]

    def z_copies(self):
        return [
            self.copy(6, self.z_send.at[0], self.z_recv.at[0], 2, 1),
            self.copy(7, self.z_send.at[1], self.z_recv.at[1], 2, -1),
        ]

    def own_part(self):
        inner = self.cells_y
        for f in range(5):
            source = self.disp.at[f] if f < 3 else (self.mass, self.energy)[f - 3]
            self.held[f, :, inner:, :] = jnp.zeros(
                (self.cells_x + 2, self.rows - inner, LANES), f32
            )
            self.held[f, 1 : self.cells_x + 1, 0:inner, :] = source[...]

    def y_start(self):
        slabs = self.cells_x + 2
        for f in range(5):
            for i in range(slabs):
                self.y_send[f, i : i + 1, :] = self.held[f, i, self.cells_y - 1 : self.cells_y, :]
                if f < 3:
                    self.y_send[5 + f, i : i + 1, :] = self.held[f, i, 0:1, :]
        for copy in self.y_copies():
            copy.start()

    def z_start(self):
        slabs, rows = self.cells_x + 2, self.rows
        lane = iota((rows, LANES), 1)
        up, down = jnp.zeros((rows, LANES), f32), jnp.zeros((rows, LANES), f32)
        for f in range(5):
            for i in range(slabs):
                self.held[f, i, rows - 1 : rows, :] = self.y_recv[f, i : i + 1, :]
                if f < 3:
                    self.held[f, i, self.cells_y : self.cells_y + 1, :] = self.y_recv[
                        5 + f, i : i + 1, :
                    ]
                slab = self.held[f, i]
                up = jnp.where(lane == f * 24 + i, slab[:, LANES - 1 : LANES], up)
                if f < 3:
                    down = jnp.where(lane == f * 24 + i, slab[:, 0:1], down)
        self.z_send[0] = up
        self.z_send[1] = down
        for copy in self.z_copies():
            copy.start()

    def zone_forces(self, out):
        rows, cells_x, cells_y = self.rows, self.cells_x, self.cells_y
        lane, row = iota((rows, LANES), 1), iota((rows, LANES), 0)
        limits = [
            self.sizes[0] * cells_x - 2,
            self.sizes[1] * cells_y - 2,
            self.sizes[2] * LANES - 2,
        ]
        at_x = self.at[0] * cells_x
        at_y = self.at[1] * cells_y + jnp.where(row < cells_y, row, row - rows)
        at_z = self.at[2] * LANES + lane
        inside_y = (at_y >= 0) & (at_y <= limits[1])
        inside_yz = inside_y & (at_z <= limits[2])

        def packed(plane, f):
            return plane if f == 0 else pltpu.roll(plane, LANES - 24 * f, 1)

        below, own = self.z_recv[0], self.z_send[1]
        low = [z_and_y_sums(packed(below, c), packed(own, c), rows) for c in range(3)]
        high = [[pltpu.roll(part, LANES - 1, 1) for part in parts] for parts in low]
        i_at = at_x + lane - 1
        valid = inside_y & (i_at >= 0) & (i_at <= limits[0]) & (self.at[2] > 0)
        thin = zone_terms(low, high, packed(below, 3), packed(below, 4), valid)

        above = self.z_recv[1]

        def slab_sums(i):
            sums = []
            for c in range(3):
                near = self.held[c, i]
                q = c * 24 + i
                far = jnp.where(
                    lane == LANES - 1, above[:, q : q + 1], pltpu.roll(near, LANES - 1, 1)
                )
                sums.append(z_and_y_sums(near, far, rows))
            return sums

        low = slab_sums(0)
        for i in range(cells_x + 1):
            high = slab_sums(i + 1)
            i_at = at_x + (i - 1)
            valid = inside_yz & (i_at >= 0) & (i_at <= limits[0])
            terms = zone_terms(low, high, self.held[3, i], self.held[4, i], valid)
            for c in range(3):
                here = [terms[a][c] for a in range(3)]
                back = [
                    jnp.where(lane == 0, thin[a][c][:, i : i + 1], pltpu.roll(here[a], 1, 1))
                    for a in range(3)
                ]
                sum_x, sum_y, sum_z = here[0] + back[0], here[1] + back[1], back[2] - here[2]
                along = sum_x + pltpu.roll(sum_x, 1, 0)
                aside = pltpu.roll(sum_y + sum_z, 1, 0) + (sum_z - sum_y)
                if i < cells_x:
                    out[c, i * cells_y : (i + 1) * cells_y, :] = (aside + along)[0:cells_y]
                if i > 0:
                    out[c, (i - 1) * cells_y : i * cells_y, :] += (aside - along)[0:cells_y]
            low = high


def exchange_kernel(
    sizes,
    disp,
    mass,
    energy,
    spos,
    sstiff,
    sactive,
    peer,
    block,
    mnode,
    marea,
    factive,
    push_out,
    total_out,
    place_out,
    zone_out,
    ask_send,
    ask_recv,
    give_send,
    give_recv,
    back_send,
    back_recv,
    slave,
    centers,
    table,
    hot_t,
    held,
    y_send,
    y_recv,
    z_send,
    z_recv,
    ask_sems,
    give_sems,
    back_sems,
    halo_sems,
):
    size_y, size_z = sizes[1:]
    halo = Halo(disp, mass, energy, held, y_send, y_recv, z_send, z_recv, halo_sems, sizes)
    peers = size_y * size_z
    count = peer.shape[1]
    masters = mnode.shape[0]
    gx, gy, gz = lax.axis_index("gx"), lax.axis_index("gy"), lax.axis_index("gz")

    def device_ahead(t):
        return (gx, lax.rem(gy + t // size_z, size_y), lax.rem(gz + t % size_z, size_z))

    def device_behind(t):
        return (
            gx,
            lax.rem(gy + size_y - t // size_z, size_y),
            lax.rem(gz + size_z - t % size_z, size_z),
        )

    barrier = pltpu.get_barrier_semaphore()

    def greet(t, carry):
        pl.semaphore_signal(barrier, inc=1, device_id=device_ahead(t), device_id_type=MESH)
        return carry

    lax.fori_loop(1, peers, greet, 0)
    for shift in (1, -1):
        pl.semaphore_signal(
            barrier, inc=1, device_id=halo.beside(0, shift), device_id_type=MESH
        )

    named = peer[...]
    ahead = lax.rem(named // size_z - gy + size_y, size_y) * size_z + lax.rem(
        named % size_z - gz + size_z, size_z
    )
    to_peer = (ahead == iota((peers, count), 0)).astype(f32)
    before = (iota((count, count), 0) < iota((count, count), 1)).astype(f32).astype(bf16)
    rank = jnp.sum(to_peer * dot(to_peer.astype(bf16), before), axis=0, keepdims=True).astype(i32)
    place = ahead * SLOTS + rank
    place_out[...] = jnp.broadcast_to(place, place_out.shape)
    in_rank = jnp.where(rank == iota((LANES, count), 0), (block[...] + 1).astype(f32), 0.0)
    asked = lax.dot_general(
        to_peer.astype(bf16), in_rank.astype(bf16), NT, preferred_element_type=f32
    )
    for t in range(peers):
        ask_send[t] = asked[t : t + 1, :]
    ask_recv[0] = asked[0:1, :]

    pl.semaphore_wait(barrier, peers + 1)

    def ask_copy(t):
        return pltpu.make_async_remote_copy(
            src_ref=ask_send.at[t],
            dst_ref=ask_recv.at[t],
            send_sem=ask_sems.at[0, t],
            recv_sem=ask_sems.at[1, t],
            device_id=device_ahead(t),
            device_id_type=MESH,
        )

    def give_copy(t):
        return pltpu.make_async_remote_copy(
            src_ref=give_send.at[t],
            dst_ref=give_recv.at[t],
            send_sem=give_sems.at[0, t],
            recv_sem=give_sems.at[1, t],
            device_id=device_behind(t),
            device_id_type=MESH,
        )

    def back_copy(t):
        return pltpu.make_async_remote_copy(
            src_ref=back_send.at[t],
            dst_ref=back_recv.at[t],
            send_sem=back_sems.at[0, t],
            recv_sem=back_sems.at[1, t],
            device_id=device_ahead(t),
            device_id_type=MESH,
        )

    def ask_start(t, carry):
        ask_copy(t).start()
        return carry

    lax.fori_loop(1, peers, ask_start, 0)
    for copy in halo.x_copies():
        copy.start()
    halo.own_part()

    gather_centers(disp, mnode, centers, table)
    live = factive[...].astype(f32)
    areas = [marea[c] * live for c in range(3)]
    moved = areas[0] * centers[0] + areas[1] * centers[1] + areas[2] * centers[2]
    pack = jnp.concatenate(areas + [moved], axis=1)
    pack3 = jnp.concatenate(split3(pack), axis=0)

    for copy in halo.x_copies():
        copy.wait_recv()
    halo.y_start()

    def ask_wait(t, carry):
        ask_copy(t).wait_recv()
        return carry

    lax.fori_loop(1, peers, ask_wait, 0)
    diagonal = (iota((peers, SLOTS, LANES), 1) == iota((peers, SLOTS, LANES), 2)).astype(f32)
    wanted = jnp.sum(
        jnp.broadcast_to(ask_recv[...], (peers, SLOTS, LANES)) * diagonal, axis=2, keepdims=True
    )
    wanted = wanted.astype(i32).reshape(peers * SLOTS, 1) - 1
    hot = (wanted == iota((peers * SLOTS, masters), 1)).astype(f32)
    hot_t[...] = jnp.transpose(
        (wanted == iota((peers * SLOTS, LANES), 1)).astype(f32)
    ).astype(bf16)
    hot3 = jnp.concatenate([hot, hot, hot], axis=1).astype(bf16)
    given = dot(hot3, pack3)
    for c in range(4):
        give_send[:, c * SLOTS : (c + 1) * SLOTS, :] = given[
            :, c * LANES : (c + 1) * LANES
        ].reshape(peers, SLOTS, LANES)

    def give_start(t, carry):
        give_copy(t).start()
        return carry

    lax.fori_loop(1, peers, give_start, 0)
    give_recv[0] = give_send[0]
    for copy in halo.y_copies():
        copy.wait_recv()
    halo.z_start()

    stiff = sstiff[...] * sactive[...].astype(f32)
    slots = (place == iota((peers * SLOTS, count), 0)).astype(f32).astype(bf16)
    for c in range(4):
        field = stiff if c == 3 else -(stiff * spos[c])
        parts = split3(field)
        rows = dot(slots, parts[0]) + dot(slots, parts[1]) + dot(slots, parts[2])
        slave[:, c * SLOTS : (c + 1) * SLOTS, :] = rows.reshape(peers, SLOTS, LANES)

    for copy in halo.z_copies():
        copy.wait_recv()
    halo.zone_forces(zone_out)

    step_of = 4

    def contact(q, carry):
        for u in range(step_of):
            t = q * step_of + u

            @pl.when(t > 0)
            def _():
                give_copy(t).wait_recv()

        for u in range(step_of):
            t = q * step_of + u
            push, total = contact_slots(give_recv[t], slave[t])
            push_out[t] = push
            back_send[t] = total
        for u in range(step_of):
            t = q * step_of + u

            @pl.when(t > 0)
            def _():
                back_copy(t).start()

        return carry

    lax.fori_loop(0, peers // step_of, contact, 0)
    back_recv[0] = back_send[0]

    def finish(t, carry):
        back_copy(t).wait_recv()
        back_copy(t).wait_send()
        give_copy(t).wait_send()
        ask_copy(t).wait_send()
        return carry

    lax.fori_loop(1, peers, finish, 0)
    for copy in halo.x_copies() + halo.y_copies() + halo.z_copies():
        copy.wait_send()
    parts = split3(back_recv[...].reshape(peers * SLOTS, LANES))
    turned = hot_t[0:masters, :]
    total_out[...] = dot(turned, parts[0]) + dot(turned, parts[1]) + dot(turned, parts[2])


def scatter_kernel(push, total, place, mnode, marea, zone, node_out, slave_out, grid):
    masters = mnode.shape[0]
    peers = push.shape[0]
    count = place.shape[1]
    rows = zone.shape[1]

    turned = jnp.transpose(place[...])
    slots = (turned[:, 0:1] == iota((count, peers * SLOTS), 1)).astype(f32).astype(bf16)
    for c in range(3):
        field = push[:, c * SLOTS : (c + 1) * SLOTS, :].reshape(peers * SLOTS, LANES)
        parts = split3(field)
        slave_out[c] = dot(slots, parts[0]) + dot(slots, parts[1]) + dot(slots, parts[2])

    row_at = iota((rows, 2 * LANES), 0)
    lane_at = iota((LANES, 2 * LANES), 0)
    grid[...] = jnp.zeros_like(grid)

    def step(q, carry):
        pair = [pl.ds(2 * q + u, 1) for u in range(2)]
        index = jnp.concatenate([mnode[at, :] for at in pair], axis=1)
        hot = (lax.shift_right_logical(index, 7) == row_at).astype(f32).astype(bf16)
        here = (index & (LANES - 1)) == lane_at
        high, low = [], []
        for c in range(3):
            force = -jnp.concatenate([marea[c, at, :] * total[at, :] for at in pair], axis=1)
            first = force.astype(bf16).astype(f32)
            high.append(jnp.where(here, first, 0.0).astype(bf16))
            low.append(jnp.where(here, force - first, 0.0).astype(bf16))
        spread = jnp.concatenate(
            [jnp.concatenate(high, axis=0), jnp.concatenate(low, axis=0)], axis=1
        )
        grid[...] += lax.dot_general(
            spread, jnp.concatenate([hot, hot], axis=1), NT, preferred_element_type=f32
        )
        return carry

    lax.fori_loop(0, masters // 2, step, 0, unroll=4)
    for c in range(3):
        node_out[c] = zone[c] + jnp.transpose(grid[c * LANES : (c + 1) * LANES, :])


def body(
    displacement,
    zone_mass,
    zone_energy,
    slave_position,
    slave_stiffness,
    slave_active,
    partner_peer,
    partner_block,
    master_node,
    master_area,
    face_active,
):
    sizes = tuple(lax.axis_size(axis) for axis in ("gx", "gy", "gz"))
    peers = sizes[1] * sizes[2]
    count = slave_position.shape[0]
    masters = master_node.shape[0]
    cells = displacement.shape[1:]
    rows = cells[0] * cells[1]
    area = jnp.transpose(master_area, (1, 0, 2))
    push, total, place, zone = pl.pallas_call(
        functools.partial(exchange_kernel, sizes),
        out_shape=(
            jax.ShapeDtypeStruct((peers, 24, LANES), f32),
            jax.ShapeDtypeStruct((masters, LANES), f32),
            jax.ShapeDtypeStruct((8, count), i32),
            jax.ShapeDtypeStruct((3, rows, LANES), f32),
        ),
        in_specs=[VMEM] * 11,
        out_specs=(VMEM,) * 4,
        scratch_shapes=[
            pltpu.VMEM((peers, 1, LANES), f32),
            pltpu.VMEM((peers, 1, LANES), f32),
            pltpu.VMEM((peers, 32, LANES), f32),
            pltpu.VMEM((peers, 32, LANES), f32),
            pltpu.VMEM((peers, 8, LANES), f32),
            pltpu.VMEM((peers, 8, LANES), f32),
            pltpu.VMEM((peers, 32, LANES), f32),
            pltpu.VMEM((3, masters, LANES), f32),
            pltpu.VMEM((3 * LANES, 3 * rows), bf16),
            pltpu.VMEM((LANES, peers * SLOTS), bf16),
            pltpu.VMEM((5, cells[0] + 2, cells[1] + 8, LANES), f32),
            pltpu.VMEM((8, cells[0] + 8, LANES), f32),
            pltpu.VMEM((8, cells[0] + 8, LANES), f32),
            pltpu.VMEM((2, cells[1] + 8, LANES), f32),
            pltpu.VMEM((2, cells[1] + 8, LANES), f32),
            pltpu.SemaphoreType.DMA((2, peers)),
            pltpu.SemaphoreType.DMA((2, peers)),
            pltpu.SemaphoreType.DMA((2, peers)),
            pltpu.SemaphoreType.DMA((2, 8)),
        ],
        compiler_params=pltpu.CompilerParams(
            collective_id=0, has_side_effects=True, vmem_limit_bytes=48 * 2**20
        ),
        name="exchange",
    )(
        displacement,
        zone_mass,
        zone_energy,
        jnp.transpose(slave_position, (1, 0, 2)),
        slave_stiffness,
        slave_active,
        partner_peer.reshape(1, count),
        partner_block.reshape(1, count),
        master_node,
        area,
        face_active,
    )
    node_force, slave_force = pl.pallas_call(
        scatter_kernel,
        out_shape=(
            jax.ShapeDtypeStruct((3, rows, LANES), f32),
            jax.ShapeDtypeStruct((3, count, LANES), f32),
        ),
        in_specs=[VMEM] * 6,
        out_specs=(VMEM,) * 2,
        scratch_shapes=[pltpu.VMEM((3 * LANES, rows), f32)],
        compiler_params=pltpu.CompilerParams(vmem_limit_bytes=48 * 2**20),
        name="scatter",
    )(push, total, place, master_node, area, zone)
    return (
        node_force.reshape((3,) + cells),
        jnp.transpose(slave_force, (1, 0, 2)),
    )


def solution(mesh):
    return jax.shard_map(
        body,
        mesh=mesh,
        in_specs=(
            P(None, "gx", "gy", "gz"),
            P("gx", "gy", "gz"),
            P("gx", "gy", "gz"),
            P(("gx", "gy", "gz"), None, None),
            P(("gx", "gy", "gz"), None),
            P(("gx", "gy", "gz"), None),
            P(("gx", "gy", "gz"), None),
            P(("gx", "gy", "gz"), None),
            P(("gx", "gy", "gz"), None),
            P(("gx", "gy", "gz"), None, None),
            P(("gx", "gy", "gz"), None),
        ),
        out_specs=(P(None, "gx", "gy", "gz"), P(("gx", "gy", "gz"), None, None)),
        check_vma=False,
    )
```

```python
import functools

import jax
import jax.numpy as jnp
from jax import lax
from jax.experimental import pallas as pl
from jax.experimental.pallas import tpu as pltpu
from jax.sharding import PartitionSpec as P

f32 = jnp.float32
bf16 = jnp.bfloat16
i32 = jnp.int32
NT = (((1,), (1,)), ((), ()))
MESH = pl.DeviceIdType.MESH
VMEM = pl.BlockSpec(memory_space=pltpu.VMEM)
HBM = pl.BlockSpec(memory_space=pltpu.HBM)
SLOTS = 8
LANES = 128

gamma_gas = 5.0 / 3.0


def split3(x):
    first = x.astype(bf16)
    rest = x - first.astype(f32)
    second = rest.astype(bf16)
    third = (rest - second.astype(f32)).astype(bf16)
    return first, second, third


def dot(left, right):
    return jnp.dot(left, right, preferred_element_type=f32)


def iota(shape, axis):
    return lax.broadcasted_iota(i32, shape, axis)


def gather_centers(disp, mnode, centers, table):
    rows = disp.shape[1] * disp.shape[2]
    for c in range(3):
        turned = jnp.transpose(disp[c].reshape(rows, LANES))
        for s, part in enumerate(split3(turned)):
            table[c * LANES : (c + 1) * LANES, s * rows : (s + 1) * rows] = part
    row_at = iota((rows, 2 * LANES), 0)
    lane_at = iota((LANES, 2 * LANES), 0)

    def step(q, carry):
        index = jnp.concatenate([mnode[pl.ds(2 * q + u, 1), :] for u in range(2)], axis=1)
        hot = (lax.shift_right_logical(index, 7) == row_at).astype(f32).astype(bf16)
        picked = dot(table[...], jnp.concatenate([hot, hot, hot], axis=0))
        here = (index & (LANES - 1)) == lane_at
        for c in range(3):
            row = jnp.sum(
                jnp.where(here, picked[c * LANES : (c + 1) * LANES], 0.0), axis=0, keepdims=True
            )
            for u in range(2):
                centers[c, pl.ds(2 * q + u, 1), :] = row[:, u * LANES : (u + 1) * LANES]
        return carry

    lax.fori_loop(0, mnode.shape[0] // 2, step, 0, unroll=4)


def contact_slots(master, slave):
    m1, m2, m3 = [part.astype(f32) for part in split3(master)]
    s1, s2, s3 = [part.astype(f32) for part in split3(slave)]
    zero = jnp.zeros_like(master)
    turned = jnp.concatenate(
        [
            jnp.transpose(jnp.concatenate([m1, m2, m3, m1], axis=0)),
            jnp.transpose(jnp.concatenate([m2, m1, zero, zero], axis=0)),
        ],
        axis=1,
    ).astype(bf16)
    weights = jnp.concatenate([s1, s1, s1, s2, s2, s3, zero, zero], axis=0)
    slot_row = iota((256, LANES), 0) & (SLOTS - 1)
    areas = jnp.concatenate([m1[:24], zero[:8], m2[:24], zero[:8]], axis=0).astype(bf16)
    areas = jnp.concatenate([areas, areas], axis=1)
    push_row = iota((64, LANES), 0) & (SLOTS - 1)
    push = jnp.zeros((64, LANES), f32)
    columns = []
    for q in range(SLOTS // 2):
        chosen = jnp.concatenate(
            [jnp.where(slot_row == 2 * q + u, weights, 0.0).astype(bf16) for u in range(2)], axis=1
        )
        depth = jnp.maximum(dot(turned, chosen), 0.0)
        high = depth.astype(bf16)
        low = (depth - high.astype(f32)).astype(bf16)
        sums = dot(areas, jnp.concatenate([high, low], axis=0))
        for u in range(2):
            half = slice(u * LANES, (u + 1) * LANES)
            push = jnp.where(push_row == 2 * q + u, sums[:, half], push)
            columns.append(jnp.sum(depth[:, half], axis=1, keepdims=True))
    return push[:24] + push[32:56], jnp.transpose(jnp.concatenate(columns, axis=1))


def cross_parts(left, right):
    return [
        left[1] * right[2] - left[2] * right[1],
        left[2] * right[0] - left[0] * right[2],
        left[0] * right[1] - left[1] * right[0],
    ]


def z_and_y_sums(near, far, rows):
    total, change = near + far, far - near
    total_up = pltpu.roll(total, rows - 1, 0)
    change_up = pltpu.roll(change, rows - 1, 0)
    return total + total_up, total_up - total, change + change_up


def zone_terms(low, high, mass, energy, valid):
    edge_x = [0.25 * (high[c][0] - low[c][0]) + (1.0 if c == 0 else 0.0) for c in range(3)]
    edge_y = [0.25 * (low[c][1] + high[c][1]) + (1.0 if c == 1 else 0.0) for c in range(3)]
    edge_z = [0.25 * (low[c][2] + high[c][2]) + (1.0 if c == 2 else 0.0) for c in range(3)]
    across_yz = cross_parts(edge_y, edge_z)
    across_zx = cross_parts(edge_z, edge_x)
    across_xy = cross_parts(edge_x, edge_y)
    volume = edge_x[0] * across_yz[0] + edge_x[1] * across_yz[1] + edge_x[2] * across_yz[2]
    pressure = jnp.where(
        valid, (gamma_gas - 1.0) * mass * energy / jnp.where(valid, volume, 1.0), 0.0
    )
    quarter = 0.25 * pressure
    return [[quarter * part for part in parts] for parts in (across_yz, across_zx, across_xy)]


class Halo:
    def __init__(self, disp, mass, energy, held, y_send, y_recv, z_send, z_recv, sems, sizes):
        self.disp, self.mass, self.energy, self.held = disp, mass, energy, held
        self.y_send, self.y_recv, self.z_send, self.z_recv = y_send, y_recv, z_send, z_recv
        self.sems, self.sizes = sems, sizes
        self.at = [lax.axis_index(axis) for axis in ("gx", "gy", "gz")]
        self.cells_x, self.cells_y = disp.shape[1], disp.shape[2]
        self.rows = held.shape[2]

    def beside(self, axis, shift):
        place = list(self.at)
        place[axis] = lax.rem(place[axis] + self.sizes[axis] + shift, self.sizes[axis])
        return tuple(place)

    def copy(self, number, source, target, axis, shift):
        return pltpu.make_async_remote_copy(
            src_ref=source,
            dst_ref=target,
            send_sem=self.sems.at[0, number],
            recv_sem=self.sems.at[1, number],
            device_id=self.beside(axis, shift),
            device_id_type=MESH,
        )

    def x_copies(self):
        last, own = self.cells_x - 1, pl.ds(0, self.cells_y)
        return [
            self.copy(0, self.disp.at[:, last], self.held.at[pl.ds(0, 3), 0, own], 0, 1),
            self.copy(1, self.mass.at[last], self.held.at[3, 0, own], 0, 1),
            self.copy(2, self.energy.at[last], self.held.at[4, 0, own], 0, 1),
            self.copy(3, self.disp.at[:, 0], self.held.at[pl.ds(0, 3), last + 2, own], 0, -1),
        ]

    def y_copies(self):
        return [
            self.copy(4, self.y_send.at[pl.ds(0, 5)], self.y_recv.at[pl.ds(0, 5)], 1, 1),
            self.copy(5, self.y_send.at[pl.ds(5, 3)], self.y_recv.at[pl.ds(5, 3)], 1, -1),
        ]

    def z_copies(self):
        return [
            self.copy(6, self.z_send.at[0], self.z_recv.at[0], 2, 1),
            self.copy(7, self.z_send.at[1], self.z_recv.at[1], 2, -1),
        ]

    def own_part(self):
        inner = self.cells_y
        for f in range(5):
            source = self.disp.at[f] if f < 3 else (self.mass, self.energy)[f - 3]
            self.held[f, :, inner:, :] = jnp.zeros(
                (self.cells_x + 2, self.rows - inner, LANES), f32
            )
            self.held[f, 1 : self.cells_x + 1, 0:inner, :] = source[...]

    def y_start(self):
        slabs = self.cells_x + 2
        for f in range(5):
            for i in range(slabs):
                self.y_send[f, i : i + 1, :] = self.held[f, i, self.cells_y - 1 : self.cells_y, :]
                if f < 3:
                    self.y_send[5 + f, i : i + 1, :] = self.held[f, i, 0:1, :]
        for copy in self.y_copies():
            copy.start()

    def z_start(self):
        slabs, rows = self.cells_x + 2, self.rows
        lane = iota((rows, LANES), 1)
        up, down = jnp.zeros((rows, LANES), f32), jnp.zeros((rows, LANES), f32)
        for f in range(5):
            for i in range(slabs):
                self.held[f, i, rows - 1 : rows, :] = self.y_recv[f, i : i + 1, :]
                if f < 3:
                    self.held[f, i, self.cells_y : self.cells_y + 1, :] = self.y_recv[
                        5 + f, i : i + 1, :
                    ]
                slab = self.held[f, i]
                up = jnp.where(lane == f * 24 + i, slab[:, LANES - 1 : LANES], up)
                if f < 3:
                    down = jnp.where(lane == f * 24 + i, slab[:, 0:1], down)
        self.z_send[0] = up
        self.z_send[1] = down
        for copy in self.z_copies():
            copy.start()

    def zone_forces(self, out):
        rows, cells_x, cells_y = self.rows, self.cells_x, self.cells_y
        lane, row = iota((rows, LANES), 1), iota((rows, LANES), 0)
        limits = [
            self.sizes[0] * cells_x - 2,
            self.sizes[1] * cells_y - 2,
            self.sizes[2] * LANES - 2,
        ]
        at_x = self.at[0] * cells_x
        at_y = self.at[1] * cells_y + jnp.where(row < cells_y, row, row - rows)
        at_z = self.at[2] * LANES + lane
        inside_y = (at_y >= 0) & (at_y <= limits[1])
        inside_yz = inside_y & (at_z <= limits[2])

        def packed(plane, f):
            return plane if f == 0 else pltpu.roll(plane, LANES - 24 * f, 1)

        below, own = self.z_recv[0], self.z_send[1]
        low = [z_and_y_sums(packed(below, c), packed(own, c), rows) for c in range(3)]
        high = [[pltpu.roll(part, LANES - 1, 1) for part in parts] for parts in low]
        i_at = at_x + lane - 1
        valid = inside_y & (i_at >= 0) & (i_at <= limits[0]) & (self.at[2] > 0)
        thin = zone_terms(low, high, packed(below, 3), packed(below, 4), valid)

        above = self.z_recv[1]

        def slab_sums(i):
            sums = []
            for c in range(3):
                near = self.held[c, i]
                q = c * 24 + i
                far = jnp.where(
                    lane == LANES - 1, above[:, q : q + 1], pltpu.roll(near, LANES - 1, 1)
                )
                sums.append(z_and_y_sums(near, far, rows))
            return sums

        low = slab_sums(0)
        for i in range(cells_x + 1):
            high = slab_sums(i + 1)
            i_at = at_x + (i - 1)
            valid = inside_yz & (i_at >= 0) & (i_at <= limits[0])
            terms = zone_terms(low, high, self.held[3, i], self.held[4, i], valid)
            for c in range(3):
                here = [terms[a][c] for a in range(3)]
                back = [
                    jnp.where(lane == 0, thin[a][c][:, i : i + 1], pltpu.roll(here[a], 1, 1))
                    for a in range(3)
                ]
                sum_x, sum_y, sum_z = here[0] + back[0], here[1] + back[1], back[2] - here[2]
                along = sum_x + pltpu.roll(sum_x, 1, 0)
                aside = pltpu.roll(sum_y + sum_z, 1, 0) + (sum_z - sum_y)
                if i < cells_x:
                    out[c, i * cells_y : (i + 1) * cells_y, :] = (aside + along)[0:cells_y]
                if i > 0:
                    out[c, (i - 1) * cells_y : i * cells_y, :] += (aside - along)[0:cells_y]
            low = high


def split_refs(refs, counts):
    groups, at = [], 0
    for count in counts:
        groups.append(refs[at : at + count])
        at += count
    return groups


def exchange_kernel(sizes, *refs):
    (
        inputs,
        (push_out, total_out, place_out, zone_out),
        locals_,
        (ask_send, ask_recv, packs, give_send, give_recv, back_send, back_recv, sum_send, sum_recv),
        (slave, centers, table, hot, hot_t),
        (held, y_send, y_recv, z_send, z_recv),
        (in_sems, ask_sems, ring_sems, give_sems, back_sems, sum_sems, halo_sems),
    ) = split_refs(refs, (11, 4, 11, 9, 5, 5, 7))
    disp, mass, energy, spos, sstiff, sactive, peer, block, mnode, marea, factive = locals_
    size_y, size_z = sizes[1:]
    peers = size_y * size_z
    count = peer.shape[1]
    masters = mnode.shape[0]
    gx, gy, gz = lax.axis_index("gx"), lax.axis_index("gy"), lax.axis_index("gz")
    halo = Halo(disp, mass, energy, held, y_send, y_recv, z_send, z_recv, halo_sems, sizes)

    def load(n):
        return pltpu.make_async_copy(inputs[n], locals_[n], in_sems.at[n])

    for n in range(11):
        load(n).start()

    def along_y(shift):
        return (gx, lax.rem(gy + shift + size_y, size_y), gz)

    def along_z(shift):
        return (gx, gy, lax.rem(gz + shift + size_z, size_z))

    barrier = pltpu.get_barrier_semaphore()
    greeted = [along_y(n) for n in range(1, size_y)] + [along_z(n) for n in range(1, size_z)]
    greeted += [halo.beside(0, 1), halo.beside(0, -1)]
    for device in greeted:
        pl.semaphore_signal(barrier, inc=1, device_id=device, device_id_type=MESH)

    def z_shift(b):
        return jnp.where(b % 2 == 1, -((b + 1) // 2), b // 2)

    for n in range(11):
        load(n).wait()

    named = peer[...]
    aside = lax.rem(named // size_z - gy + size_y, size_y)
    away = lax.rem(named % size_z - gz + size_z, size_z)
    batch = jnp.where(away < size_z // 2, 2 * away, 2 * (size_z - away) - 1)
    to_peer = (aside * size_z + batch == iota((peers, count), 0)).astype(f32)
    before = (iota((count, count), 0) < iota((count, count), 1)).astype(f32).astype(bf16)
    rank = jnp.sum(to_peer * dot(to_peer.astype(bf16), before), axis=0, keepdims=True).astype(i32)
    place = (batch * size_y + aside) * SLOTS + rank
    place_out[...] = jnp.broadcast_to(place, place_out.shape)
    in_rank = jnp.where(rank == iota((LANES, count), 0), (block[...] + 1).astype(f32), 0.0)
    asked = lax.dot_general(
        to_peer.astype(bf16), in_rank.astype(bf16), NT, preferred_element_type=f32
    )
    for t in range(peers):
        ask_send[t] = asked[t : t + 1, :]
    ask_recv[0:size_z] = ask_send[0:size_z]

    pl.semaphore_wait(barrier, len(greeted))

    def ask_copy(n):
        rows = pl.ds(n * size_z, size_z)
        return pltpu.make_async_remote_copy(
            src_ref=ask_send.at[rows],
            dst_ref=ask_recv.at[rows],
            send_sem=ask_sems.at[0, n],
            recv_sem=ask_sems.at[1, n],
            device_id=along_y(n),
            device_id_type=MESH,
        )

    half = masters // 2

    def ring_copy(step, up):
        side = 0 if up else 1
        source = 0 if step == 0 else 2 * step - 1 + side
        target = 2 * step + 1 + side
        if step == size_z // 2 - 1:
            rows, target = pl.ds(side * half, half), size_z - 1
        else:
            rows = pl.ds(0, masters)
        return pltpu.make_async_remote_copy(
            src_ref=packs.at[source, rows],
            dst_ref=packs.at[target, rows],
            send_sem=ring_sems.at[0, side, step],
            recv_sem=ring_sems.at[1, side, step],
            device_id=along_z(1 if up else -1),
            device_id_type=MESH,
        )

    def give_copy(b, n):
        t = b * size_y + n
        return pltpu.make_async_remote_copy(
            src_ref=give_send.at[t],
            dst_ref=give_recv.at[t],
            send_sem=give_sems.at[0, t],
            recv_sem=give_sems.at[1, t],
            device_id=along_y(-n),
            device_id_type=MESH,
        )

    def back_copy(b, n):
        t = b * size_y + n
        return pltpu.make_async_remote_copy(
            src_ref=back_send.at[t],
            dst_ref=back_recv.at[t],
            send_sem=back_sems.at[0, t],
            recv_sem=back_sems.at[1, t],
            device_id=along_y(n),
            device_id_type=MESH,
        )

    def sum_copy(b):
        return pltpu.make_async_remote_copy(
            src_ref=sum_send.at[b],
            dst_ref=sum_recv.at[b],
            send_sem=sum_sems.at[0, b],
            recv_sem=sum_sems.at[1, b],
            device_id=along_z(z_shift(b)),
            device_id_type=MESH,
        )

    for n in range(1, size_y):
        ask_copy(n).start()
    for copy in halo.x_copies():
        copy.start()
    halo.own_part()

    gather_centers(disp, mnode, centers, table)
    live = factive[...].astype(f32)
    areas = [marea[c] * live for c in range(3)]
    moved = areas[0] * centers[0] + areas[1] * centers[1] + areas[2] * centers[2]
    packs[0] = jnp.concatenate(areas + [moved], axis=1)
    ring_copy(0, True).start()
    ring_copy(0, False).start()

    for copy in halo.x_copies():
        copy.wait_recv()
    halo.y_start()

    for n in range(1, size_y):
        ask_copy(n).wait_recv()
    diagonal = (iota((peers, SLOTS, LANES), 1) == iota((peers, SLOTS, LANES), 2)).astype(f32)
    wanted = jnp.sum(
        jnp.broadcast_to(ask_recv[...], (peers, SLOTS, LANES)) * diagonal, axis=2, keepdims=True
    )
    picked = (wanted.astype(i32) - 1 == iota((peers, SLOTS, LANES), 2)).astype(f32)
    hot[...] = picked.reshape(size_y, size_z, SLOTS, LANES)
    for b in range(size_z):
        chosen = hot[:, b].reshape(size_y * SLOTS, LANES)
        hot_t[b] = jnp.transpose(chosen)[0:masters].astype(bf16)

    def give(b):
        chosen = hot[:, b].reshape(size_y * SLOTS, LANES)[:, 0:masters]
        chosen = jnp.concatenate([chosen, chosen, chosen], axis=1).astype(bf16)
        given = dot(chosen, jnp.concatenate(split3(packs[b]), axis=0))
        for c in range(4):
            give_send[b * size_y : (b + 1) * size_y, c * SLOTS : (c + 1) * SLOTS, :] = given[
                :, c * LANES : (c + 1) * LANES
            ].reshape(size_y, SLOTS, LANES)
        for n in range(1, size_y):
            give_copy(b, n).start()
        give_recv[b * size_y] = give_send[b * size_y]

    give(0)
    for copy in halo.y_copies():
        copy.wait_recv()
    halo.z_start()

    stiff = sstiff[...] * sactive[...].astype(f32)
    slots = (place == iota((peers * SLOTS, count), 0)).astype(f32).astype(bf16)
    for c in range(4):
        field = stiff if c == 3 else -(stiff * spos[c])
        parts = split3(field)
        rows = dot(slots, parts[0]) + dot(slots, parts[1]) + dot(slots, parts[2])
        slave[:, c * SLOTS : (c + 1) * SLOTS, :] = rows.reshape(peers, SLOTS, LANES)

    for copy in halo.z_copies():
        copy.wait_recv()
    halo.zone_forces(zone_out)

    def ring_step(step):
        last = step == size_z // 2 - 1
        for up in (True, False):
            ring_copy(step, up).wait_recv()
            if not last:
                ring_copy(step + 1, up).start()
        for b in (2 * step + 1, 2 * step + 2):
            if b < size_z:
                give(b)

    def summed(b):
        for n in range(1, size_y):
            back_copy(b, n).wait_recv()
        rows = back_recv[pl.ds(b * size_y, size_y)].reshape(size_y * SLOTS, LANES)
        parts = split3(rows)
        turned = hot_t[b]
        sum_send[b] = dot(turned, parts[0]) + dot(turned, parts[1]) + dot(turned, parts[2])

        @pl.when(b > 0)
        def _():
            sum_copy(b).start()

    step_of = 4
    parts_of = size_y // step_of

    def contact(q, carry):
        for step in range(size_z // 2):

            @pl.when(q == 3 * step)
            def _():
                ring_step(step)

        @pl.when((q % parts_of == 0) & (q >= 2 * parts_of))
        def _():
            summed(q // parts_of - 2)

        b = q // parts_of
        for u in range(step_of):
            n = (q % parts_of) * step_of + u

            @pl.when(n > 0)
            def _():
                give_copy(b, n).wait_recv()

        for u in range(step_of):
            t = q * step_of + u
            push, total = contact_slots(give_recv[t], slave[t])
            push_out[t] = push
            back_send[t] = total
        for u in range(step_of):
            n = (q % parts_of) * step_of + u

            @pl.when(n > 0)
            def _():
                back_copy(b, n).start()

            @pl.when(n == 0)
            def _():
                back_recv[b * size_y] = back_send[b * size_y]

        return carry

    lax.fori_loop(0, size_z * parts_of, contact, 0)
    summed(size_z - 2)
    summed(size_z - 1)

    def sent(b, carry):
        for n in range(1, size_y):
            give_copy(b, n).wait_send()
            back_copy(b, n).wait_send()
        return carry

    lax.fori_loop(0, size_z, sent, 0)
    for n in range(1, size_y):
        ask_copy(n).wait_send()
    for step in range(size_z // 2):
        ring_copy(step, True).wait_send()
        ring_copy(step, False).wait_send()
    for copy in halo.x_copies() + halo.y_copies() + halo.z_copies():
        copy.wait_send()
    total = sum_send[0]
    for b in range(1, size_z):
        sum_copy(b).wait_recv()
        sum_copy(b).wait_send()
        total = total + sum_recv[b]
    total_out[...] = total


def scatter_kernel(push, total, place, mnode, marea, zone, node_out, slave_out, grid):
    masters = mnode.shape[0]
    peers = push.shape[0]
    count = place.shape[1]
    rows = zone.shape[1]

    turned = jnp.transpose(place[...])
    slots = (turned[:, 0:1] == iota((count, peers * SLOTS), 1)).astype(f32).astype(bf16)
    for c in range(3):
        field = push[:, c * SLOTS : (c + 1) * SLOTS, :].reshape(peers * SLOTS, LANES)
        parts = split3(field)
        slave_out[c] = dot(slots, parts[0]) + dot(slots, parts[1]) + dot(slots, parts[2])

    row_at = iota((rows, 2 * LANES), 0)
    lane_at = iota((LANES, 2 * LANES), 0)
    grid[...] = jnp.zeros_like(grid)

    def step(q, carry):
        pair = [pl.ds(2 * q + u, 1) for u in range(2)]
        index = jnp.concatenate([mnode[at, :] for at in pair], axis=1)
        hot = (lax.shift_right_logical(index, 7) == row_at).astype(f32).astype(bf16)
        here = (index & (LANES - 1)) == lane_at
        high, low = [], []
        for c in range(3):
            force = -jnp.concatenate([marea[c, at, :] * total[at, :] for at in pair], axis=1)
            first = force.astype(bf16).astype(f32)
            high.append(jnp.where(here, first, 0.0).astype(bf16))
            low.append(jnp.where(here, force - first, 0.0).astype(bf16))
        spread = jnp.concatenate(
            [jnp.concatenate(high, axis=0), jnp.concatenate(low, axis=0)], axis=1
        )
        grid[...] += lax.dot_general(
            spread, jnp.concatenate([hot, hot], axis=1), NT, preferred_element_type=f32
        )
        return carry

    lax.fori_loop(0, masters // 2, step, 0, unroll=4)
    for c in range(3):
        node_out[c] = zone[c] + jnp.transpose(grid[c * LANES : (c + 1) * LANES, :])


def body(
    displacement,
    zone_mass,
    zone_energy,
    slave_position,
    slave_stiffness,
    slave_active,
    partner_peer,
    partner_block,
    master_node,
    master_area,
    face_active,
):
    sizes = tuple(lax.axis_size(axis) for axis in ("gx", "gy", "gz"))
    peers = sizes[1] * sizes[2]
    count = slave_position.shape[0]
    masters = master_node.shape[0]
    cells = displacement.shape[1:]
    rows = cells[0] * cells[1]
    area = jnp.transpose(master_area, (1, 0, 2))
    push, total, place, zone = pl.pallas_call(
        functools.partial(exchange_kernel, sizes),
        out_shape=(
            jax.ShapeDtypeStruct((peers, 24, LANES), f32),
            jax.ShapeDtypeStruct((masters, LANES), f32),
            jax.ShapeDtypeStruct((8, count), i32),
            jax.ShapeDtypeStruct((3, rows, LANES), f32),
        ),
        in_specs=[HBM] * 11,
        out_specs=(VMEM,) * 4,
        scratch_shapes=[
            pltpu.VMEM(displacement.shape, f32),
            pltpu.VMEM(zone_mass.shape, f32),
            pltpu.VMEM(zone_energy.shape, f32),
            pltpu.VMEM((3, count, LANES), f32),
            pltpu.VMEM((count, LANES), f32),
            pltpu.VMEM((count, LANES), i32),
            pltpu.VMEM((1, count), i32),
            pltpu.VMEM((1, count), i32),
            pltpu.VMEM((masters, LANES), i32),
            pltpu.VMEM((3, masters, LANES), f32),
            pltpu.VMEM((masters, LANES), i32),
            pltpu.VMEM((peers, 1, LANES), f32),
            pltpu.VMEM((peers, 1, LANES), f32),
            pltpu.VMEM((sizes[2], masters, 4 * LANES), f32),
            pltpu.VMEM((peers, 32, LANES), f32),
            pltpu.VMEM((peers, 32, LANES), f32),
            pltpu.VMEM((peers, 8, LANES), f32),
            pltpu.VMEM((peers, 8, LANES), f32),
            pltpu.VMEM((sizes[2], masters, LANES), f32),
            pltpu.VMEM((sizes[2], masters, LANES), f32),
            pltpu.VMEM((peers, 32, LANES), f32),
            pltpu.VMEM((3, masters, LANES), f32),
            pltpu.VMEM((3 * LANES, 3 * rows), bf16),
            pltpu.VMEM((sizes[1], sizes[2], SLOTS, LANES), f32),
            pltpu.VMEM((sizes[2], masters, sizes[1] * SLOTS), bf16),
            pltpu.VMEM((5, cells[0] + 2, cells[1] + 8, LANES), f32),
            pltpu.VMEM((8, cells[0] + 8, LANES), f32),
            pltpu.VMEM((8, cells[0] + 8, LANES), f32),
            pltpu.VMEM((2, cells[1] + 8, LANES), f32),
            pltpu.VMEM((2, cells[1] + 8, LANES), f32),
            pltpu.SemaphoreType.DMA((11,)),
            pltpu.SemaphoreType.DMA((2, sizes[1])),
            pltpu.SemaphoreType.DMA((2, 2, sizes[2] // 2)),
            pltpu.SemaphoreType.DMA((2, peers)),
            pltpu.SemaphoreType.DMA((2, peers)),
            pltpu.SemaphoreType.DMA((2, sizes[2])),
            pltpu.SemaphoreType.DMA((2, 8)),
        ],
        compiler_params=pltpu.CompilerParams(
            collective_id=0, has_side_effects=True, vmem_limit_bytes=48 * 2**20
        ),
        name="exchange",
    )(
        displacement,
        zone_mass,
        zone_energy,
        jnp.transpose(slave_position, (1, 0, 2)),
        slave_stiffness,
        slave_active,
        partner_peer.reshape(1, count),
        partner_block.reshape(1, count),
        master_node,
        area,
        face_active,
    )
    node_force, slave_force = pl.pallas_call(
        scatter_kernel,
        out_shape=(
            jax.ShapeDtypeStruct((3, rows, LANES), f32),
            jax.ShapeDtypeStruct((3, count, LANES), f32),
        ),
        in_specs=[VMEM] * 6,
        out_specs=(VMEM,) * 2,
        scratch_shapes=[pltpu.VMEM((3 * LANES, rows), f32)],
        compiler_params=pltpu.CompilerParams(vmem_limit_bytes=48 * 2**20),
        name="scatter",
    )(push, total, place, master_node, area, zone)
    return (
        node_force.reshape((3,) + cells),
        jnp.transpose(slave_force, (1, 0, 2)),
    )


def solution(mesh):
    return jax.shard_map(
        body,
        mesh=mesh,
        in_specs=(
            P(None, "gx", "gy", "gz"),
            P("gx", "gy", "gz"),
            P("gx", "gy", "gz"),
            P(("gx", "gy", "gz"), None, None),
            P(("gx", "gy", "gz"), None),
            P(("gx", "gy", "gz"), None),
            P(("gx", "gy", "gz"), None),
            P(("gx", "gy", "gz"), None),
            P(("gx", "gy", "gz"), None),
            P(("gx", "gy", "gz"), None, None),
            P(("gx", "gy", "gz"), None),
        ),
        out_specs=(P(None, "gx", "gy", "gz"), P(("gx", "gy", "gz"), None, None)),
        check_vma=False,
    )
```

```python
import functools

import jax
import jax.numpy as jnp
from jax import lax
from jax.experimental import pallas as pl
from jax.experimental.pallas import tpu as pltpu
from jax.sharding import PartitionSpec as P

f32 = jnp.float32
bf16 = jnp.bfloat16
i32 = jnp.int32
NT = (((1,), (1,)), ((), ()))
MESH = pl.DeviceIdType.MESH
VMEM = pl.BlockSpec(memory_space=pltpu.VMEM)
HBM = pl.BlockSpec(memory_space=pltpu.HBM)
SLOTS = 8
LANES = 128

gamma_gas = 5.0 / 3.0


def split3(x):
    first = x.astype(bf16)
    rest = x - first.astype(f32)
    second = rest.astype(bf16)
    third = (rest - second.astype(f32)).astype(bf16)
    return first, second, third


def dot(left, right):
    return jnp.dot(left, right, preferred_element_type=f32)


def iota(shape, axis):
    return lax.broadcasted_iota(i32, shape, axis)


def gather_centers(disp, mnode, centers, table):
    rows = disp.shape[1] * disp.shape[2]
    for c in range(3):
        turned = jnp.transpose(disp[c].reshape(rows, LANES))
        for s, part in enumerate(split3(turned)[:2]):
            table[c * LANES : (c + 1) * LANES, s * rows : (s + 1) * rows] = part
    row_at = iota((rows, 2 * LANES), 0)
    lane_at = iota((LANES, 2 * LANES), 0)

    def step(q, carry):
        index = jnp.concatenate([mnode[pl.ds(2 * q + u, 1), :] for u in range(2)], axis=1)
        hot = (lax.shift_right_logical(index, 7) == row_at).astype(f32).astype(bf16)
        picked = dot(table[...], jnp.concatenate([hot, hot], axis=0))
        here = (index & (LANES - 1)) == lane_at
        for c in range(3):
            row = jnp.sum(
                jnp.where(here, picked[c * LANES : (c + 1) * LANES], 0.0), axis=0, keepdims=True
            )
            for u in range(2):
                centers[c, pl.ds(2 * q + u, 1), :] = row[:, u * LANES : (u + 1) * LANES]
        return carry

    lax.fori_loop(0, mnode.shape[0] // 2, step, 0, unroll=8)


def contact_slots(master, slave):
    m1, m2, m3 = [part.astype(f32) for part in split3(master)]
    s1, s2, s3 = [part.astype(f32) for part in split3(slave)]
    zero = jnp.zeros_like(master)
    turned = jnp.concatenate(
        [
            jnp.transpose(jnp.concatenate([m1, m2, m3, m1], axis=0)),
            jnp.transpose(jnp.concatenate([m2, m1, zero, zero], axis=0)),
        ],
        axis=1,
    ).astype(bf16)
    weights = jnp.concatenate([s1, s1, s1, s2, s2, s3, zero, zero], axis=0)
    slot_row = iota((256, LANES), 0) & (SLOTS - 1)
    areas = jnp.concatenate([m1[:24], zero[:8], m2[:24], zero[:8]], axis=0).astype(bf16)
    areas = jnp.concatenate([areas, areas], axis=1)
    push_row = iota((64, LANES), 0) & (SLOTS - 1)
    push = jnp.zeros((64, LANES), f32)
    columns = []
    for q in range(SLOTS // 2):
        chosen = jnp.concatenate(
            [jnp.where(slot_row == 2 * q + u, weights, 0.0).astype(bf16) for u in range(2)], axis=1
        )
        depth = jnp.maximum(dot(turned, chosen), 0.0)
        high = depth.astype(bf16)
        low = (depth - high.astype(f32)).astype(bf16)
        sums = dot(areas, jnp.concatenate([high, low], axis=0))
        for u in range(2):
            half = slice(u * LANES, (u + 1) * LANES)
            push = jnp.where(push_row == 2 * q + u, sums[:, half], push)
            columns.append(jnp.sum(depth[:, half], axis=1, keepdims=True))
    return push[:24] + push[32:56], jnp.transpose(jnp.concatenate(columns, axis=1))


def cross_parts(left, right):
    return [
        left[1] * right[2] - left[2] * right[1],
        left[2] * right[0] - left[0] * right[2],
        left[0] * right[1] - left[1] * right[0],
    ]


def z_and_y_sums(near, far, rows):
    total, change = near + far, far - near
    total_up = pltpu.roll(total, rows - 1, 0)
    change_up = pltpu.roll(change, rows - 1, 0)
    return total + total_up, total_up - total, change + change_up


def zone_terms(low, high, mass, energy, valid):
    edge_x = [0.25 * (high[c][0] - low[c][0]) + (1.0 if c == 0 else 0.0) for c in range(3)]
    edge_y = [0.25 * (low[c][1] + high[c][1]) + (1.0 if c == 1 else 0.0) for c in range(3)]
    edge_z = [0.25 * (low[c][2] + high[c][2]) + (1.0 if c == 2 else 0.0) for c in range(3)]
    across_yz = cross_parts(edge_y, edge_z)
    across_zx = cross_parts(edge_z, edge_x)
    across_xy = cross_parts(edge_x, edge_y)
    volume = edge_x[0] * across_yz[0] + edge_x[1] * across_yz[1] + edge_x[2] * across_yz[2]
    pressure = jnp.where(
        valid, (gamma_gas - 1.0) * mass * energy / jnp.where(valid, volume, 1.0), 0.0
    )
    quarter = 0.25 * pressure
    return [[quarter * part for part in parts] for parts in (across_yz, across_zx, across_xy)]


class Halo:
    def __init__(self, disp, mass, energy, held, y_send, y_recv, z_send, z_recv, sems, sizes):
        self.disp, self.mass, self.energy, self.held = disp, mass, energy, held
        self.y_send, self.y_recv, self.z_send, self.z_recv = y_send, y_recv, z_send, z_recv
        self.sems, self.sizes = sems, sizes
        self.at = [lax.axis_index(axis) for axis in ("gx", "gy", "gz")]
        self.cells_x, self.cells_y = disp.shape[1], disp.shape[2]
        self.rows = held.shape[2]

    def beside(self, axis, shift):
        place = list(self.at)
        place[axis] = lax.rem(place[axis] + self.sizes[axis] + shift, self.sizes[axis])
        return tuple(place)

    def copy(self, number, source, target, axis, shift):
        return pltpu.make_async_remote_copy(
            src_ref=source,
            dst_ref=target,
            send_sem=self.sems.at[0, number],
            recv_sem=self.sems.at[1, number],
            device_id=self.beside(axis, shift),
            device_id_type=MESH,
        )

    def x_copies(self):
        last, own = self.cells_x - 1, pl.ds(0, self.cells_y)
        return [
            self.copy(0, self.disp.at[:, last], self.held.at[pl.ds(0, 3), 0, own], 0, 1),
            self.copy(1, self.mass.at[last], self.held.at[3, 0, own], 0, 1),
            self.copy(2, self.energy.at[last], self.held.at[4, 0, own], 0, 1),
            self.copy(3, self.disp.at[:, 0], self.held.at[pl.ds(0, 3), last + 2, own], 0, -1),
        ]

    def y_copies(self):
        return [
            self.copy(4, self.y_send.at[pl.ds(0, 5)], self.y_recv.at[pl.ds(0, 5)], 1, 1),
            self.copy(5, self.y_send.at[pl.ds(5, 3)], self.y_recv.at[pl.ds(5, 3)], 1, -1),
        ]

    def z_copies(self):
        return [
            self.copy(6, self.z_send.at[0], self.z_recv.at[0], 2, 1),
            self.copy(7, self.z_send.at[1], self.z_recv.at[1], 2, -1),
        ]

    def own_part(self):
        inner = self.cells_y
        for f in range(5):
            source = self.disp.at[f] if f < 3 else (self.mass, self.energy)[f - 3]
            self.held[f, :, inner:, :] = jnp.zeros(
                (self.cells_x + 2, self.rows - inner, LANES), f32
            )
            self.held[f, 1 : self.cells_x + 1, 0:inner, :] = source[...]

    def y_start(self):
        slabs = self.cells_x + 2
        for f in range(5):
            for i in range(slabs):
                self.y_send[f, i : i + 1, :] = self.held[f, i, self.cells_y - 1 : self.cells_y, :]
                if f < 3:
                    self.y_send[5 + f, i : i + 1, :] = self.held[f, i, 0:1, :]
        for copy in self.y_copies():
            copy.start()

    def z_start(self):
        slabs, rows = self.cells_x + 2, self.rows
        lane = iota((rows, LANES), 1)
        up, down = jnp.zeros((rows, LANES), f32), jnp.zeros((rows, LANES), f32)
        for f in range(5):
            for i in range(slabs):
                self.held[f, i, rows - 1 : rows, :] = self.y_recv[f, i : i + 1, :]
                if f < 3:
                    self.held[f, i, self.cells_y : self.cells_y + 1, :] = self.y_recv[
                        5 + f, i : i + 1, :
                    ]
                slab = self.held[f, i]
                up = jnp.where(lane == f * 24 + i, slab[:, LANES - 1 : LANES], up)
                if f < 3:
                    down = jnp.where(lane == f * 24 + i, slab[:, 0:1], down)
        self.z_send[0] = up
        self.z_send[1] = down
        for copy in self.z_copies():
            copy.start()

    def zone_forces(self, out):
        rows, cells_x, cells_y = self.rows, self.cells_x, self.cells_y
        lane, row = iota((rows, LANES), 1), iota((rows, LANES), 0)
        limits = [
            self.sizes[0] * cells_x - 2,
            self.sizes[1] * cells_y - 2,
            self.sizes[2] * LANES - 2,
        ]
        at_x = self.at[0] * cells_x
        at_y = self.at[1] * cells_y + jnp.where(row < cells_y, row, row - rows)
        at_z = self.at[2] * LANES + lane
        inside_y = (at_y >= 0) & (at_y <= limits[1])
        inside_yz = inside_y & (at_z <= limits[2])

        def packed(plane, f):
            return plane if f == 0 else pltpu.roll(plane, LANES - 24 * f, 1)

        below, own = self.z_recv[0], self.z_send[1]
        low = [z_and_y_sums(packed(below, c), packed(own, c), rows) for c in range(3)]
        high = [[pltpu.roll(part, LANES - 1, 1) for part in parts] for parts in low]
        i_at = at_x + lane - 1
        valid = inside_y & (i_at >= 0) & (i_at <= limits[0]) & (self.at[2] > 0)
        thin = zone_terms(low, high, packed(below, 3), packed(below, 4), valid)

        above = self.z_recv[1]

        def slab_sums(i):
            sums = []
            for c in range(3):
                near = self.held[c, i]
                q = c * 24 + i
                far = jnp.where(
                    lane == LANES - 1, above[:, q : q + 1], pltpu.roll(near, LANES - 1, 1)
                )
                sums.append(z_and_y_sums(near, far, rows))
            return sums

        low = slab_sums(0)
        for i in range(cells_x + 1):
            high = slab_sums(i + 1)
            i_at = at_x + (i - 1)
            valid = inside_yz & (i_at >= 0) & (i_at <= limits[0])
            terms = zone_terms(low, high, self.held[3, i], self.held[4, i], valid)
            for c in range(3):
                here = [terms[a][c] for a in range(3)]
                back = [
                    jnp.where(lane == 0, thin[a][c][:, i : i + 1], pltpu.roll(here[a], 1, 1))
                    for a in range(3)
                ]
                sum_x, sum_y, sum_z = here[0] + back[0], here[1] + back[1], back[2] - here[2]
                along = sum_x + pltpu.roll(sum_x, 1, 0)
                aside = pltpu.roll(sum_y + sum_z, 1, 0) + (sum_z - sum_y)
                if i < cells_x:
                    out[c, i * cells_y : (i + 1) * cells_y, :] = (aside + along)[0:cells_y]
                if i > 0:
                    out[c, (i - 1) * cells_y : i * cells_y, :] += (aside - along)[0:cells_y]
            low = high
            if i == cells_x // 2:
                yield
        yield


def slave_forces(push, place, slave_out):
    count, slots_of = place.shape[1], push.shape[0] * SLOTS
    turned = jnp.transpose(jnp.broadcast_to(place, (8, count)))
    slots = (turned[:, 0:1] == iota((count, slots_of), 1)).astype(f32).astype(bf16)
    for c in range(3):
        field = push[:, c * SLOTS : (c + 1) * SLOTS, :].reshape(slots_of, LANES)
        parts = split3(field)
        slave_out[c] = dot(slots, parts[0]) + dot(slots, parts[1]) + dot(slots, parts[2])


def add_reactions(total, mnode, marea, zone, node_out, grid):
    masters, rows = mnode.shape[0], zone.shape[1]
    row_at = iota((rows, 2 * LANES), 0)
    lane_at = iota((LANES, 2 * LANES), 0)
    grid[...] = jnp.zeros_like(grid)

    def step(q, carry):
        pair = [pl.ds(2 * q + u, 1) for u in range(2)]
        index = jnp.concatenate([mnode[at, :] for at in pair], axis=1)
        hot = (lax.shift_right_logical(index, 7) == row_at).astype(f32).astype(bf16)
        here = (index & (LANES - 1)) == lane_at
        high, low = [], []
        for c in range(3):
            force = -jnp.concatenate([marea[c, at, :] * total[at, :] for at in pair], axis=1)
            first = force.astype(bf16).astype(f32)
            high.append(jnp.where(here, first, 0.0).astype(bf16))
            low.append(jnp.where(here, force - first, 0.0).astype(bf16))
        spread = jnp.concatenate(
            [jnp.concatenate(high, axis=0), jnp.concatenate(low, axis=0)], axis=1
        )
        grid[...] += lax.dot_general(
            spread, jnp.concatenate([hot, hot], axis=1), NT, preferred_element_type=f32
        )
        return carry

    lax.fori_loop(0, masters // 2, step, 0, unroll=8)
    for c in range(3):
        node_out[c] = zone[c] + jnp.transpose(grid[c * LANES : (c + 1) * LANES, :])


def split_refs(refs, counts):
    groups, at = [], 0
    for count in counts:
        groups.append(refs[at : at + count])
        at += count
    return groups


def exchange_kernel(sizes, *refs):
    (
        inputs,
        (node_out, slave_out),
        locals_,
        (ask_send, ask_recv, packs, give_send, give_recv, back_send, back_recv, sum_send, sum_recv),
        (slave, centers, table, hot, hot_t, push_out, total_out, zone_out, grid),
        (held, y_send, y_recv, z_send, z_recv),
        (in_sems, ask_sems, ring_sems, give_sems, back_sems, sum_sems, halo_sems),
    ) = split_refs(refs, (11, 2, 11, 9, 9, 5, 7))
    disp, mass, energy, spos, sstiff, sactive, peer, block, mnode, marea, factive = locals_
    size_y, size_z = sizes[1:]
    peers = size_y * size_z
    count = peer.shape[1]
    masters = mnode.shape[0]
    gx, gy, gz = lax.axis_index("gx"), lax.axis_index("gy"), lax.axis_index("gz")
    halo = Halo(disp, mass, energy, held, y_send, y_recv, z_send, z_recv, halo_sems, sizes)

    def load(n):
        return pltpu.make_async_copy(inputs[n], locals_[n], in_sems.at[n])

    for n in (6, 7, 0, 8, 1, 2, 9, 10, 4, 5, 3):
        load(n).start()

    def along_y(shift):
        return (gx, lax.rem(gy + shift + size_y, size_y), gz)

    def along_z(shift):
        return (gx, gy, lax.rem(gz + shift + size_z, size_z))

    barrier = pltpu.get_barrier_semaphore()
    greeted = size_y + size_z

    def greet_y(n, carry):
        pl.semaphore_signal(barrier, inc=1, device_id=along_y(n), device_id_type=MESH)
        return carry

    def greet_z(n, carry):
        pl.semaphore_signal(barrier, inc=1, device_id=along_z(n), device_id_type=MESH)
        return carry

    lax.fori_loop(1, size_y, greet_y, 0)
    lax.fori_loop(1, size_z, greet_z, 0)
    for side in (1, -1):
        pl.semaphore_signal(
            barrier, inc=1, device_id=halo.beside(0, side), device_id_type=MESH
        )

    def z_shift(b):
        return jnp.where(b % 2 == 1, -((b + 1) // 2), b // 2)

    for n in (6, 7):
        load(n).wait()

    named = peer[...]
    aside = lax.rem(named // size_z - gy + size_y, size_y)
    away = lax.rem(named % size_z - gz + size_z, size_z)
    batch = jnp.where(away < size_z // 2, 2 * away, 2 * (size_z - away) - 1)
    to_peer = (aside * size_z + batch == iota((peers, count), 0)).astype(f32)
    before = (iota((count, count), 0) < iota((count, count), 1)).astype(f32).astype(bf16)
    rank = jnp.sum(to_peer * dot(to_peer.astype(bf16), before), axis=0, keepdims=True).astype(i32)
    place = (batch * size_y + aside) * SLOTS + rank
    in_rank = jnp.where(rank == iota((LANES, count), 0), (block[...] + 1).astype(f32), 0.0)
    asked = lax.dot_general(
        to_peer.astype(bf16), in_rank.astype(bf16), NT, preferred_element_type=f32
    )
    for t in range(peers):
        ask_send[t] = asked[t : t + 1, :]
    ask_recv[0:size_z] = ask_send[0:size_z]

    for n in (0, 1, 2):
        load(n).wait()
    pl.semaphore_wait(barrier, greeted)

    def ask_copy(n):
        rows = pl.ds(n * size_z, size_z)
        return pltpu.make_async_remote_copy(
            src_ref=ask_send.at[rows],
            dst_ref=ask_recv.at[rows],
            send_sem=ask_sems.at[0, n],
            recv_sem=ask_sems.at[1, n],
            device_id=along_y(n),
            device_id_type=MESH,
        )

    half = masters // 2

    def ring_copy(step, up, chunk):
        side = 0 if up else 1
        source = 0 if step == 0 else 2 * step - 1 + side
        target = 2 * step + 1 + side
        if step == size_z // 2 - 1:
            target = size_z - 1
        rows = pl.ds(chunk * half, half)
        return pltpu.make_async_remote_copy(
            src_ref=packs.at[source, rows],
            dst_ref=packs.at[target, rows],
            send_sem=ring_sems.at[0, side, step, chunk],
            recv_sem=ring_sems.at[1, side, step, chunk],
            device_id=along_z(1 if up else -1),
            device_id_type=MESH,
        )

    def ring_copies(step):
        if step == size_z // 2 - 1:
            return [(True, 0), (False, 1)]
        return [(True, 0), (False, 1), (True, 1), (False, 0)]

    def give_copy(b, n):
        t = b * size_y + n
        return pltpu.make_async_remote_copy(
            src_ref=give_send.at[t],
            dst_ref=give_recv.at[t],
            send_sem=give_sems.at[0, t],
            recv_sem=give_sems.at[1, t],
            device_id=along_y(-n),
            device_id_type=MESH,
        )

    def back_copy(b, n):
        t = b * size_y + n
        return pltpu.make_async_remote_copy(
            src_ref=back_send.at[t],
            dst_ref=back_recv.at[t],
            send_sem=back_sems.at[0, t],
            recv_sem=back_sems.at[1, t],
            device_id=along_y(n),
            device_id_type=MESH,
        )

    def sum_copy(b):
        return pltpu.make_async_remote_copy(
            src_ref=sum_send.at[b],
            dst_ref=sum_recv.at[b],
            send_sem=sum_sems.at[0, b],
            recv_sem=sum_sems.at[1, b],
            device_id=along_z(z_shift(b)),
            device_id_type=MESH,
        )

    def each(n, carry):
        ask_copy(n).start()
        return carry

    lax.fori_loop(1, size_y, each, 0)
    for copy in halo.x_copies():
        copy.start()
    for n in (8, 9, 10):
        load(n).wait()
    gather_centers(disp, mnode, centers, table)
    live = factive[...].astype(f32)
    areas = [marea[c] * live for c in range(3)]
    moved = areas[0] * centers[0] + areas[1] * centers[1] + areas[2] * centers[2]
    packs[0] = jnp.concatenate(areas + [moved], axis=1)
    for way in ring_copies(0):
        ring_copy(0, *way).start()

    def each(n, carry):
        ask_copy(n).wait_recv()
        return carry

    lax.fori_loop(1, size_y, each, 0)
    diagonal = (iota((peers, SLOTS, LANES), 1) == iota((peers, SLOTS, LANES), 2)).astype(f32)
    wanted = jnp.sum(
        jnp.broadcast_to(ask_recv[...], (peers, SLOTS, LANES)) * diagonal, axis=2, keepdims=True
    )
    picked = (wanted.astype(i32) - 1 == iota((peers, SLOTS, LANES), 2)).astype(f32)
    hot[...] = picked.reshape(size_y, size_z, SLOTS, LANES)
    for b in range(size_z):
        chosen = hot[:, b].reshape(size_y * SLOTS, LANES)
        hot_t[b] = jnp.transpose(chosen)[0:masters].astype(bf16)

    def give(b):
        chosen = hot[:, b].reshape(size_y * SLOTS, LANES)[:, 0:masters]
        chosen = jnp.concatenate([chosen, chosen, chosen], axis=1).astype(bf16)
        given = dot(chosen, jnp.concatenate(split3(packs[b]), axis=0))
        for c in range(4):
            give_send[b * size_y : (b + 1) * size_y, c * SLOTS : (c + 1) * SLOTS, :] = given[
                :, c * LANES : (c + 1) * LANES
            ].reshape(size_y, SLOTS, LANES)
        def each(n, carry):
            give_copy(b, n).start()
            return carry

        lax.fori_loop(1, size_y, each, 0)
        give_recv[b * size_y] = give_send[b * size_y]

    give(0)
    halo.own_part()
    for copy in halo.x_copies():
        copy.wait_recv()
    halo.y_start()
    for n in (3, 4, 5):
        load(n).wait()

    stiff = sstiff[...] * sactive[...].astype(f32)
    slots = (place == iota((peers * SLOTS, count), 0)).astype(f32).astype(bf16)
    for c in range(4):
        field = stiff if c == 3 else -(stiff * spos[c])
        parts = split3(field)
        rows = dot(slots, parts[0]) + dot(slots, parts[1]) + dot(slots, parts[2])
        slave[:, c * SLOTS : (c + 1) * SLOTS, :] = rows.reshape(peers, SLOTS, LANES)

    for copy in halo.y_copies():
        copy.wait_recv()
    halo.z_start()

    def ring_step(step):
        for way in ring_copies(step):
            ring_copy(step, *way).wait_recv()
            if step < size_z // 2 - 1 and way in ring_copies(step + 1):
                ring_copy(step + 1, *way).start()
        for b in (2 * step + 1, 2 * step + 2):
            if b < size_z:
                give(b)

    def summed(b):
        def each(n, carry):
            back_copy(b, n).wait_recv()
            return carry

        lax.fori_loop(1, size_y, each, 0)
        rows = back_recv[pl.ds(b * size_y, size_y)].reshape(size_y * SLOTS, LANES)
        parts = split3(rows)
        turned = hot_t[b]
        sum_send[b] = dot(turned, parts[0]) + dot(turned, parts[1]) + dot(turned, parts[2])

        @pl.when(b > 0)
        def _():
            sum_copy(b).start()

    step_of = 4
    parts_of = size_y // step_of

    def contact(q, carry):
        for step in range(size_z // 2):

            @pl.when(q == 3 * step)
            def _():
                ring_step(step)

        @pl.when((q % parts_of == 0) & (q >= 2 * parts_of))
        def _():
            summed(q // parts_of - 2)

        b = q // parts_of
        for u in range(step_of):
            n = (q % parts_of) * step_of + u

            @pl.when(n > 0)
            def _():
                give_copy(b, n).wait_recv()

        for u in range(step_of):
            t = q * step_of + u
            push, total = contact_slots(give_recv[t], slave[t])
            push_out[t] = push
            back_send[t] = total
        for u in range(step_of):
            n = (q % parts_of) * step_of + u

            @pl.when(n > 0)
            def _():
                back_copy(b, n).start()

            @pl.when(n == 0)
            def _():
                back_recv[b * size_y] = back_send[b * size_y]

        return carry

    lax.fori_loop(0, size_z * parts_of, contact, 0)
    summed(size_z - 2)
    for copy in halo.z_copies():
        copy.wait_recv()
    forces = halo.zone_forces(zone_out)
    next(forces)
    slave_forces(push_out, place, slave_out)
    summed(size_z - 1)
    next(forces)

    def sent(b, carry):
        def each(n, carry):
            give_copy(b, n).wait_send()
            back_copy(b, n).wait_send()
            return carry

        lax.fori_loop(1, size_y, each, 0)
        return carry

    lax.fori_loop(0, size_z, sent, 0)
    def each(n, carry):
        ask_copy(n).wait_send()
        return carry

    lax.fori_loop(1, size_y, each, 0)
    for step in range(size_z // 2):
        for way in ring_copies(step):
            ring_copy(step, *way).wait_send()
    for copy in halo.x_copies() + halo.y_copies() + halo.z_copies():
        copy.wait_send()
    total = sum_send[0]
    for b in range(1, size_z):
        sum_copy(b).wait_recv()
        sum_copy(b).wait_send()
        total = total + sum_recv[b]
    total_out[...] = total
    add_reactions(total_out, mnode, marea, zone_out, node_out, grid)


def body(
    displacement,
    zone_mass,
    zone_energy,
    slave_position,
    slave_stiffness,
    slave_active,
    partner_peer,
    partner_block,
    master_node,
    master_area,
    face_active,
):
    sizes = tuple(lax.axis_size(axis) for axis in ("gx", "gy", "gz"))
    peers = sizes[1] * sizes[2]
    count = slave_position.shape[0]
    masters = master_node.shape[0]
    cells = displacement.shape[1:]
    rows = cells[0] * cells[1]
    area = jnp.transpose(master_area, (1, 0, 2))
    node_force, slave_force = pl.pallas_call(
        functools.partial(exchange_kernel, sizes),
        out_shape=(
            jax.ShapeDtypeStruct((3, rows, LANES), f32),
            jax.ShapeDtypeStruct((3, count, LANES), f32),
        ),
        in_specs=[HBM] * 11,
        out_specs=(VMEM,) * 2,
        scratch_shapes=[
            pltpu.VMEM(displacement.shape, f32),
            pltpu.VMEM(zone_mass.shape, f32),
            pltpu.VMEM(zone_energy.shape, f32),
            pltpu.VMEM((3, count, LANES), f32),
            pltpu.VMEM((count, LANES), f32),
            pltpu.VMEM((count, LANES), i32),
            pltpu.VMEM((1, count), i32),
            pltpu.VMEM((1, count), i32),
            pltpu.VMEM((masters, LANES), i32),
            pltpu.VMEM((3, masters, LANES), f32),
            pltpu.VMEM((masters, LANES), i32),
            pltpu.VMEM((peers, 1, LANES), f32),
            pltpu.VMEM((peers, 1, LANES), f32),
            pltpu.VMEM((sizes[2], masters, 4 * LANES), f32),
            pltpu.VMEM((peers, 32, LANES), f32),
            pltpu.VMEM((peers, 32, LANES), f32),
            pltpu.VMEM((peers, 8, LANES), f32),
            pltpu.VMEM((peers, 8, LANES), f32),
            pltpu.VMEM((sizes[2], masters, LANES), f32),
            pltpu.VMEM((sizes[2], masters, LANES), f32),
            pltpu.VMEM((peers, 32, LANES), f32),
            pltpu.VMEM((3, masters, LANES), f32),
            pltpu.VMEM((3 * LANES, 2 * rows), bf16),
            pltpu.VMEM((sizes[1], sizes[2], SLOTS, LANES), f32),
            pltpu.VMEM((sizes[2], masters, sizes[1] * SLOTS), bf16),
            pltpu.VMEM((peers, 24, LANES), f32),
            pltpu.VMEM((masters, LANES), f32),
            pltpu.VMEM((3, rows, LANES), f32),
            pltpu.VMEM((3 * LANES, rows), f32),
            pltpu.VMEM((5, cells[0] + 2, cells[1] + 8, LANES), f32),
            pltpu.VMEM((8, cells[0] + 8, LANES), f32),
            pltpu.VMEM((8, cells[0] + 8, LANES), f32),
            pltpu.VMEM((2, cells[1] + 8, LANES), f32),
            pltpu.VMEM((2, cells[1] + 8, LANES), f32),
            pltpu.SemaphoreType.DMA((11,)),
            pltpu.SemaphoreType.DMA((2, sizes[1])),
            pltpu.SemaphoreType.DMA((2, 2, sizes[2] // 2, 2)),
            pltpu.SemaphoreType.DMA((2, peers)),
            pltpu.SemaphoreType.DMA((2, peers)),
            pltpu.SemaphoreType.DMA((2, sizes[2])),
            pltpu.SemaphoreType.DMA((2, 8)),
        ],
        compiler_params=pltpu.CompilerParams(
            collective_id=0, has_side_effects=True, vmem_limit_bytes=63 * 2**20
        ),
        name="exchange",
    )(
        displacement,
        zone_mass,
        zone_energy,
        jnp.transpose(slave_position, (1, 0, 2)),
        slave_stiffness,
        slave_active,
        partner_peer.reshape(1, count),
        partner_block.reshape(1, count),
        master_node,
        area,
        face_active,
    )
    return (
        node_force.reshape((3,) + cells),
        jnp.transpose(slave_force, (1, 0, 2)),
    )


def solution(mesh):
    return jax.shard_map(
        body,
        mesh=mesh,
        in_specs=(
            P(None, "gx", "gy", "gz"),
            P("gx", "gy", "gz"),
            P("gx", "gy", "gz"),
            P(("gx", "gy", "gz"), None, None),
            P(("gx", "gy", "gz"), None),
            P(("gx", "gy", "gz"), None),
            P(("gx", "gy", "gz"), None),
            P(("gx", "gy", "gz"), None),
            P(("gx", "gy", "gz"), None),
            P(("gx", "gy", "gz"), None, None),
            P(("gx", "gy", "gz"), None),
        ),
        out_specs=(P(None, "gx", "gy", "gz"), P(("gx", "gy", "gz"), None, None)),
        check_vma=False,
    )
```

```python
import functools

import jax
import jax.numpy as jnp
from jax import lax
from jax.experimental import pallas as pl
from jax.experimental.pallas import tpu as pltpu
from jax.sharding import PartitionSpec as P

f32 = jnp.float32
bf16 = jnp.bfloat16
i32 = jnp.int32
NT = (((1,), (1,)), ((), ()))
MESH = pl.DeviceIdType.MESH
VMEM = pl.BlockSpec(memory_space=pltpu.VMEM)
HBM = pl.BlockSpec(memory_space=pltpu.HBM)
SLOTS = 8
LANES = 128

gamma_gas = 5.0 / 3.0


def split3(x):
    first = x.astype(bf16)
    rest = x - first.astype(f32)
    second = rest.astype(bf16)
    third = (rest - second.astype(f32)).astype(bf16)
    return first, second, third


def dot(left, right):
    return jnp.dot(left, right, preferred_element_type=f32)


def iota(shape, axis):
    return lax.broadcasted_iota(i32, shape, axis)


def gather_centers(disp, mnode, centers, table):
    rows = disp.shape[1] * disp.shape[2]
    for c in range(3):
        turned = jnp.transpose(disp[c].reshape(rows, LANES))
        for s, part in enumerate(split3(turned)[:2]):
            table[c * LANES : (c + 1) * LANES, s * rows : (s + 1) * rows] = part
    row_at = iota((rows, 2 * LANES), 0)
    lane_at = iota((LANES, 2 * LANES), 0)

    def step(q, carry):
        index = jnp.concatenate([mnode[pl.ds(2 * q + u, 1), :] for u in range(2)], axis=1)
        hot = (lax.shift_right_logical(index, 7) == row_at).astype(f32).astype(bf16)
        picked = dot(table[...], jnp.concatenate([hot, hot], axis=0))
        here = (index & (LANES - 1)) == lane_at
        for c in range(3):
            row = jnp.sum(
                jnp.where(here, picked[c * LANES : (c + 1) * LANES], 0.0), axis=0, keepdims=True
            )
            for u in range(2):
                centers[c, pl.ds(2 * q + u, 1), :] = row[:, u * LANES : (u + 1) * LANES]
        return carry

    lax.fori_loop(0, mnode.shape[0] // 2, step, 0, unroll=8)


def contact_slots(master, slave):
    m1, m2, m3 = [part.astype(f32) for part in split3(master)]
    s1, s2, s3 = [part.astype(f32) for part in split3(slave)]
    zero = jnp.zeros_like(master)
    turned = jnp.concatenate(
        [
            jnp.transpose(jnp.concatenate([m1, m2, m3, m1], axis=0)),
            jnp.transpose(jnp.concatenate([m2, m1, zero, zero], axis=0)),
        ],
        axis=1,
    ).astype(bf16)
    weights = jnp.concatenate([s1, s1, s1, s2, s2, s3, zero, zero], axis=0)
    slot_of_row = lax.shift_right_logical(iota((256, LANES), 0), 2) & (SLOTS - 1)
    first = iota((8, LANES), 0) < 4
    pushes, columns = [], []
    for q in range(SLOTS // 2):
        chosen = jnp.concatenate(
            [jnp.where(slot_of_row == 2 * q + u, weights, 0.0).astype(bf16) for u in range(2)],
            axis=1,
        )
        depth = jnp.maximum(dot(turned, chosen), 0.0)
        high = depth.astype(bf16)
        low = (depth - high.astype(f32)).astype(bf16)
        pair = slice(8 * q, 8 * q + 8)
        areas = jnp.concatenate([m1[pair], m2[pair]], axis=0).astype(bf16)
        sums = dot(
            jnp.concatenate([areas, areas], axis=1), jnp.concatenate([high, low], axis=0)
        )
        both = sums[0:8] + sums[8:16]
        pushes.append(jnp.where(first, both[:, 0:LANES], both[:, LANES : 2 * LANES]))
        for u in range(2):
            half = slice(u * LANES, (u + 1) * LANES)
            columns.append(jnp.sum(depth[:, half], axis=1, keepdims=True))
    return jnp.concatenate(pushes, axis=0), jnp.transpose(jnp.concatenate(columns, axis=1))


def cross_parts(left, right):
    return [
        left[1] * right[2] - left[2] * right[1],
        left[2] * right[0] - left[0] * right[2],
        left[0] * right[1] - left[1] * right[0],
    ]


def z_and_y_sums(near, far, rows):
    total, change = near + far, far - near
    total_up = pltpu.roll(total, rows - 1, 0)
    change_up = pltpu.roll(change, rows - 1, 0)
    return total + total_up, total_up - total, change + change_up


def zone_terms(low, high, mass, energy, valid):
    edge_x = [0.25 * (high[c][0] - low[c][0]) + (1.0 if c == 0 else 0.0) for c in range(3)]
    edge_y = [0.25 * (low[c][1] + high[c][1]) + (1.0 if c == 1 else 0.0) for c in range(3)]
    edge_z = [0.25 * (low[c][2] + high[c][2]) + (1.0 if c == 2 else 0.0) for c in range(3)]
    across_yz = cross_parts(edge_y, edge_z)
    across_zx = cross_parts(edge_z, edge_x)
    across_xy = cross_parts(edge_x, edge_y)
    volume = edge_x[0] * across_yz[0] + edge_x[1] * across_yz[1] + edge_x[2] * across_yz[2]
    pressure = jnp.where(
        valid, (gamma_gas - 1.0) * mass * energy / jnp.where(valid, volume, 1.0), 0.0
    )
    quarter = 0.25 * pressure
    return [[quarter * part for part in parts] for parts in (across_yz, across_zx, across_xy)]


class Halo:
    def __init__(self, disp, mass, energy, held, y_send, y_recv, z_send, z_recv, sems, sizes):
        self.disp, self.mass, self.energy, self.held = disp, mass, energy, held
        self.y_send, self.y_recv, self.z_send, self.z_recv = y_send, y_recv, z_send, z_recv
        self.sems, self.sizes = sems, sizes
        self.at = [lax.axis_index(axis) for axis in ("gx", "gy", "gz")]
        self.cells_x, self.cells_y = disp.shape[1], disp.shape[2]
        self.rows = held.shape[2]

    def beside(self, axis, shift):
        place = list(self.at)
        place[axis] = lax.rem(place[axis] + self.sizes[axis] + shift, self.sizes[axis])
        return tuple(place)

    def copy(self, number, source, target, axis, shift):
        return pltpu.make_async_remote_copy(
            src_ref=source,
            dst_ref=target,
            send_sem=self.sems.at[0, number],
            recv_sem=self.sems.at[1, number],
            device_id=self.beside(axis, shift),
            device_id_type=MESH,
        )

    def x_copies(self):
        last, own = self.cells_x - 1, pl.ds(0, self.cells_y)
        return [
            self.copy(0, self.disp.at[:, last], self.held.at[pl.ds(0, 3), 0, own], 0, 1),
            self.copy(1, self.mass.at[last], self.held.at[3, 0, own], 0, 1),
            self.copy(2, self.energy.at[last], self.held.at[4, 0, own], 0, 1),
            self.copy(3, self.disp.at[:, 0], self.held.at[pl.ds(0, 3), last + 2, own], 0, -1),
        ]

    def y_copies(self):
        return [
            self.copy(4, self.y_send.at[pl.ds(0, 5)], self.y_recv.at[pl.ds(0, 5)], 1, 1),
            self.copy(5, self.y_send.at[pl.ds(5, 3)], self.y_recv.at[pl.ds(5, 3)], 1, -1),
        ]

    def z_copies(self):
        return [
            self.copy(6, self.z_send.at[0], self.z_recv.at[0], 2, 1),
            self.copy(7, self.z_send.at[1], self.z_recv.at[1], 2, -1),
        ]

    def own_part(self):
        inner = self.cells_y
        for f in range(5):
            source = self.disp.at[f] if f < 3 else (self.mass, self.energy)[f - 3]
            self.held[f, :, inner:, :] = jnp.zeros(
                (self.cells_x + 2, self.rows - inner, LANES), f32
            )
            self.held[f, 1 : self.cells_x + 1, 0:inner, :] = source[...]

    def y_start(self):
        slabs = self.cells_x + 2
        for f in range(5):
            for i in range(slabs):
                self.y_send[f, i : i + 1, :] = self.held[f, i, self.cells_y - 1 : self.cells_y, :]
                if f < 3:
                    self.y_send[5 + f, i : i + 1, :] = self.held[f, i, 0:1, :]
        for copy in self.y_copies():
            copy.start()

    def z_start(self):
        slabs, rows = self.cells_x + 2, self.rows
        lane = iota((rows, LANES), 1)
        up, down = jnp.zeros((rows, LANES), f32), jnp.zeros((rows, LANES), f32)
        for f in range(5):
            for i in range(slabs):
                self.held[f, i, rows - 1 : rows, :] = self.y_recv[f, i : i + 1, :]
                if f < 3:
                    self.held[f, i, self.cells_y : self.cells_y + 1, :] = self.y_recv[
                        5 + f, i : i + 1, :
                    ]
                slab = self.held[f, i]
                up = jnp.where(lane == f * 24 + i, slab[:, LANES - 1 : LANES], up)
                if f < 3:
                    down = jnp.where(lane == f * 24 + i, slab[:, 0:1], down)
        self.z_send[0] = up
        self.z_send[1] = down
        for copy in self.z_copies():
            copy.start()

    def zone_forces(self, out):
        rows, cells_x, cells_y = self.rows, self.cells_x, self.cells_y
        lane, row = iota((rows, LANES), 1), iota((rows, LANES), 0)
        limits = [
            self.sizes[0] * cells_x - 2,
            self.sizes[1] * cells_y - 2,
            self.sizes[2] * LANES - 2,
        ]
        at_x = self.at[0] * cells_x
        at_y = self.at[1] * cells_y + jnp.where(row < cells_y, row, row - rows)
        at_z = self.at[2] * LANES + lane
        inside_y = (at_y >= 0) & (at_y <= limits[1])
        inside_yz = inside_y & (at_z <= limits[2])

        def packed(plane, f):
            return plane if f == 0 else pltpu.roll(plane, LANES - 24 * f, 1)

        below, own = self.z_recv[0], self.z_send[1]
        low = [z_and_y_sums(packed(below, c), packed(own, c), rows) for c in range(3)]
        high = [[pltpu.roll(part, LANES - 1, 1) for part in parts] for parts in low]
        i_at = at_x + lane - 1
        valid = inside_y & (i_at >= 0) & (i_at <= limits[0]) & (self.at[2] > 0)
        thin = zone_terms(low, high, packed(below, 3), packed(below, 4), valid)

        above = self.z_recv[1]

        def slab_sums(i):
            sums = []
            for c in range(3):
                near = self.held[c, i]
                q = c * 24 + i
                far = jnp.where(
                    lane == LANES - 1, above[:, q : q + 1], pltpu.roll(near, LANES - 1, 1)
                )
                sums.append(z_and_y_sums(near, far, rows))
            return sums

        low = slab_sums(0)
        for i in range(cells_x + 1):
            high = slab_sums(i + 1)
            i_at = at_x + (i - 1)
            valid = inside_yz & (i_at >= 0) & (i_at <= limits[0])
            terms = zone_terms(low, high, self.held[3, i], self.held[4, i], valid)
            for c in range(3):
                here = [terms[a][c] for a in range(3)]
                back = [
                    jnp.where(lane == 0, thin[a][c][:, i : i + 1], pltpu.roll(here[a], 1, 1))
                    for a in range(3)
                ]
                sum_x, sum_y, sum_z = here[0] + back[0], here[1] + back[1], back[2] - here[2]
                along = sum_x + pltpu.roll(sum_x, 1, 0)
                aside = pltpu.roll(sum_y + sum_z, 1, 0) + (sum_z - sum_y)
                if i < cells_x:
                    out[c, i * cells_y : (i + 1) * cells_y, :] = (aside + along)[0:cells_y]
                if i > 0:
                    out[c, (i - 1) * cells_y : i * cells_y, :] += (aside - along)[0:cells_y]
            low = high
            if i == cells_x // 2:
                yield
        yield


def slave_forces(push, place, slave_out):
    count, slots_of = place.shape[1], push.shape[0] * SLOTS
    turned = jnp.transpose(jnp.broadcast_to(place, (8, count)))
    slots = (turned[:, 0:1] == iota((count, slots_of), 1)).astype(f32).astype(bf16)
    for c in range(3):
        field = push[:, pl.ds(c, SLOTS, stride=4), :].reshape(slots_of, LANES)
        parts = split3(field)
        slave_out[c] = dot(slots, parts[0]) + dot(slots, parts[1]) + dot(slots, parts[2])


def add_reactions(total, mnode, marea, zone, node_out, grid):
    masters, rows = mnode.shape[0], zone.shape[1]
    row_at = iota((rows, 2 * LANES), 0)
    lane_at = iota((LANES, 2 * LANES), 0)
    grid[...] = jnp.zeros_like(grid)

    def step(q, carry):
        pair = [pl.ds(2 * q + u, 1) for u in range(2)]
        index = jnp.concatenate([mnode[at, :] for at in pair], axis=1)
        hot = (lax.shift_right_logical(index, 7) == row_at).astype(f32).astype(bf16)
        here = (index & (LANES - 1)) == lane_at
        high, low = [], []
        for c in range(3):
            force = -jnp.concatenate([marea[c, at, :] * total[at, :] for at in pair], axis=1)
            first = force.astype(bf16).astype(f32)
            high.append(jnp.where(here, first, 0.0).astype(bf16))
            low.append(jnp.where(here, force - first, 0.0).astype(bf16))
        spread = jnp.concatenate(
            [jnp.concatenate(high, axis=0), jnp.concatenate(low, axis=0)], axis=1
        )
        grid[...] += lax.dot_general(
            spread, jnp.concatenate([hot, hot], axis=1), NT, preferred_element_type=f32
        )
        return carry

    lax.fori_loop(0, masters // 2, step, 0, unroll=8)
    for c in range(3):
        node_out[c] = zone[c] + jnp.transpose(grid[c * LANES : (c + 1) * LANES, :])


def split_refs(refs, counts):
    groups, at = [], 0
    for count in counts:
        groups.append(refs[at : at + count])
        at += count
    return groups


def exchange_kernel(sizes, *refs):
    (
        inputs,
        (node_out, slave_out),
        locals_,
        (ask_send, ask_recv, packs, give_send, give_recv, back_send, back_recv, sum_send, sum_recv),
        (slave, centers, table, hot, hot_t, push_out, total_out, zone_out, grid),
        (held, y_send, y_recv, z_send, z_recv),
        (in_sems, ask_sems, ring_sems, give_sems, back_sems, sum_sems, halo_sems),
    ) = split_refs(refs, (11, 2, 11, 9, 9, 5, 7))
    disp, mass, energy, spos, sstiff, sactive, peer, block, mnode, marea, factive = locals_
    size_y, size_z = sizes[1:]
    peers = size_y * size_z
    count = peer.shape[1]
    masters = mnode.shape[0]
    gx, gy, gz = lax.axis_index("gx"), lax.axis_index("gy"), lax.axis_index("gz")
    halo = Halo(disp, mass, energy, held, y_send, y_recv, z_send, z_recv, halo_sems, sizes)

    def load(n):
        return pltpu.make_async_copy(inputs[n], locals_[n], in_sems.at[n])

    for n in (6, 7, 0, 8, 1, 2, 9, 10, 4, 5, 3):
        load(n).start()

    def along_y(shift):
        return (gx, lax.rem(gy + shift + size_y, size_y), gz)

    def along_z(shift):
        return (gx, gy, lax.rem(gz + shift + size_z, size_z))

    barrier = pltpu.get_barrier_semaphore()
    greeted = size_y + size_z

    def greet_y(n, carry):
        pl.semaphore_signal(barrier, inc=1, device_id=along_y(n), device_id_type=MESH)
        return carry

    def greet_z(n, carry):
        pl.semaphore_signal(barrier, inc=1, device_id=along_z(n), device_id_type=MESH)
        return carry

    lax.fori_loop(1, size_y, greet_y, 0)
    lax.fori_loop(1, size_z, greet_z, 0)
    for side in (1, -1):
        pl.semaphore_signal(
            barrier, inc=1, device_id=halo.beside(0, side), device_id_type=MESH
        )

    def z_shift(b):
        return jnp.where(b % 2 == 1, -((b + 1) // 2), b // 2)

    for n in (6, 7):
        load(n).wait()

    named = peer[...]
    aside = lax.rem(named // size_z - gy + size_y, size_y)
    away = lax.rem(named % size_z - gz + size_z, size_z)
    batch = jnp.where(away < size_z // 2, 2 * away, 2 * (size_z - away) - 1)
    to_peer = (aside * size_z + batch == iota((peers, count), 0)).astype(f32)
    before = (iota((count, count), 0) < iota((count, count), 1)).astype(f32).astype(bf16)
    rank = jnp.sum(to_peer * dot(to_peer.astype(bf16), before), axis=0, keepdims=True).astype(i32)
    place = (batch * size_y + aside) * SLOTS + rank
    in_rank = jnp.where(rank == iota((LANES, count), 0), (block[...] + 1).astype(f32), 0.0)
    asked = lax.dot_general(
        to_peer.astype(bf16), in_rank.astype(bf16), NT, preferred_element_type=f32
    )
    for t in range(peers):
        ask_send[t] = asked[t : t + 1, :]
    ask_recv[0:size_z] = ask_send[0:size_z]

    for n in (0, 1, 2):
        load(n).wait()
    pl.semaphore_wait(barrier, greeted)

    def ask_copy(n):
        rows = pl.ds(n * size_z, size_z)
        return pltpu.make_async_remote_copy(
            src_ref=ask_send.at[rows],
            dst_ref=ask_recv.at[rows],
            send_sem=ask_sems.at[0, n],
            recv_sem=ask_sems.at[1, n],
            device_id=along_y(n),
            device_id_type=MESH,
        )

    half = masters // 2

    def ring_copy(step, up, chunk):
        side = 0 if up else 1
        source = 0 if step == 0 else 2 * step - 1 + side
        target = 2 * step + 1 + side
        if step == size_z // 2 - 1:
            target = size_z - 1
        rows = pl.ds(chunk * half, half)
        return pltpu.make_async_remote_copy(
            src_ref=packs.at[source, rows],
            dst_ref=packs.at[target, rows],
            send_sem=ring_sems.at[0, side, step, chunk],
            recv_sem=ring_sems.at[1, side, step, chunk],
            device_id=along_z(1 if up else -1),
            device_id_type=MESH,
        )

    def ring_copies(step):
        if step == size_z // 2 - 1:
            return [(True, 0), (False, 1)]
        return [(True, 0), (False, 1), (True, 1), (False, 0)]

    def give_copy(b, n):
        t = b * size_y + n
        return pltpu.make_async_remote_copy(
            src_ref=give_send.at[t],
            dst_ref=give_recv.at[t],
            send_sem=give_sems.at[0, t],
            recv_sem=give_sems.at[1, t],
            device_id=along_y(-n),
            device_id_type=MESH,
        )

    def back_copy(b, n):
        t = b * size_y + n
        return pltpu.make_async_remote_copy(
            src_ref=back_send.at[t],
            dst_ref=back_recv.at[t],
            send_sem=back_sems.at[0, t],
            recv_sem=back_sems.at[1, t],
            device_id=along_y(n),
            device_id_type=MESH,
        )

    def sum_copy(b):
        return pltpu.make_async_remote_copy(
            src_ref=sum_send.at[b],
            dst_ref=sum_recv.at[b],
            send_sem=sum_sems.at[0, b],
            recv_sem=sum_sems.at[1, b],
            device_id=along_z(z_shift(b)),
            device_id_type=MESH,
        )

    def each(n, carry):
        ask_copy(n).start()
        return carry

    lax.fori_loop(1, size_y, each, 0)
    for copy in halo.x_copies():
        copy.start()
    for n in (8, 9, 10):
        load(n).wait()
    gather_centers(disp, mnode, centers, table)
    live = factive[...].astype(f32)
    areas = [marea[c] * live for c in range(3)]
    moved = areas[0] * centers[0] + areas[1] * centers[1] + areas[2] * centers[2]
    packs[0] = jnp.concatenate(areas + [moved], axis=1)
    for way in ring_copies(0):
        ring_copy(0, *way).start()

    def each(n, carry):
        ask_copy(n).wait_recv()
        return carry

    lax.fori_loop(1, size_y, each, 0)
    diagonal = (iota((peers, SLOTS, LANES), 1) == iota((peers, SLOTS, LANES), 2)).astype(f32)
    wanted = jnp.sum(
        jnp.broadcast_to(ask_recv[...], (peers, SLOTS, LANES)) * diagonal, axis=2, keepdims=True
    )
    picked = (wanted.astype(i32) - 1 == iota((peers, SLOTS, LANES), 2)).astype(f32)
    hot[...] = picked.reshape(size_y, size_z, SLOTS, LANES)
    for b in range(size_z):
        chosen = hot[:, b].reshape(size_y * SLOTS, LANES)
        hot_t[b] = jnp.transpose(chosen)[0:masters].astype(bf16)

    def give(b):
        chosen = hot[:, b].reshape(size_y * SLOTS, LANES)[:, 0:masters]
        chosen = jnp.concatenate([chosen, chosen, chosen], axis=1).astype(bf16)
        given = dot(chosen, jnp.concatenate(split3(packs[b]), axis=0))
        for c in range(4):
            give_send[b * size_y : (b + 1) * size_y, pl.ds(c, SLOTS, stride=4), :] = given[
                :, c * LANES : (c + 1) * LANES
            ].reshape(size_y, SLOTS, LANES)
        def each(n, carry):
            give_copy(b, n).start()
            return carry

        lax.fori_loop(1, size_y, each, 0)
        give_recv[b * size_y] = give_send[b * size_y]

    give(0)
    halo.own_part()
    for copy in halo.x_copies():
        copy.wait_recv()
    halo.y_start()
    for n in (3, 4, 5):
        load(n).wait()

    stiff = sstiff[...] * sactive[...].astype(f32)
    slots = (place == iota((peers * SLOTS, count), 0)).astype(f32).astype(bf16)
    for c in range(4):
        field = stiff if c == 3 else -(stiff * spos[c])
        parts = split3(field)
        rows = dot(slots, parts[0]) + dot(slots, parts[1]) + dot(slots, parts[2])
        slave[:, pl.ds(c, SLOTS, stride=4), :] = rows.reshape(peers, SLOTS, LANES)

    for copy in halo.y_copies():
        copy.wait_recv()
    halo.z_start()

    def ring_step(step):
        for way in ring_copies(step):
            ring_copy(step, *way).wait_recv()
            if step < size_z // 2 - 1 and way in ring_copies(step + 1):
                ring_copy(step + 1, *way).start()
        for b in (2 * step + 1, 2 * step + 2):
            if b < size_z:
                give(b)

    def summed(b):
        def each(n, carry):
            back_copy(b, n).wait_recv()
            return carry

        lax.fori_loop(1, size_y, each, 0)
        rows = back_recv[pl.ds(b * size_y, size_y)].reshape(size_y * SLOTS, LANES)
        parts = split3(rows)
        turned = hot_t[b]
        sum_send[b] = dot(turned, parts[0]) + dot(turned, parts[1]) + dot(turned, parts[2])

        @pl.when(b > 0)
        def _():
            sum_copy(b).start()

    step_of = 4
    parts_of = size_y // step_of

    def contact(q, carry):
        for step in range(size_z // 2):

            @pl.when(q == 3 * step)
            def _():
                ring_step(step)

        @pl.when((q % parts_of == 0) & (q >= 2 * parts_of))
        def _():
            summed(q // parts_of - 2)

        b = q // parts_of
        for u in range(step_of):
            n = (q % parts_of) * step_of + u

            @pl.when(n > 0)
            def _():
                give_copy(b, n).wait_recv()

        for u in range(step_of):
            t = q * step_of + u
            push, total = contact_slots(give_recv[t], slave[t])
            push_out[t] = push
            back_send[t] = total
        for u in range(step_of):
            n = (q % parts_of) * step_of + u

            @pl.when(n > 0)
            def _():
                back_copy(b, n).start()

            @pl.when(n == 0)
            def _():
                back_recv[b * size_y] = back_send[b * size_y]

        return carry

    lax.fori_loop(0, size_z * parts_of, contact, 0)
    summed(size_z - 2)
    for copy in halo.z_copies():
        copy.wait_recv()
    forces = halo.zone_forces(zone_out)
    next(forces)
    slave_forces(push_out, place, slave_out)
    summed(size_z - 1)
    next(forces)

    def sent(b, carry):
        def each(n, carry):
            give_copy(b, n).wait_send()
            back_copy(b, n).wait_send()
            return carry

        lax.fori_loop(1, size_y, each, 0)
        return carry

    lax.fori_loop(0, size_z, sent, 0)
    def each(n, carry):
        ask_copy(n).wait_send()
        return carry

    lax.fori_loop(1, size_y, each, 0)
    for step in range(size_z // 2):
        for way in ring_copies(step):
            ring_copy(step, *way).wait_send()
    for copy in halo.x_copies() + halo.y_copies() + halo.z_copies():
        copy.wait_send()
    total = sum_send[0]
    for b in range(1, size_z):
        sum_copy(b).wait_recv()
        sum_copy(b).wait_send()
        total = total + sum_recv[b]
    total_out[...] = total
    add_reactions(total_out, mnode, marea, zone_out, node_out, grid)


def body(
    displacement,
    zone_mass,
    zone_energy,
    slave_position,
    slave_stiffness,
    slave_active,
    partner_peer,
    partner_block,
    master_node,
    master_area,
    face_active,
):
    sizes = tuple(lax.axis_size(axis) for axis in ("gx", "gy", "gz"))
    peers = sizes[1] * sizes[2]
    count = slave_position.shape[0]
    masters = master_node.shape[0]
    cells = displacement.shape[1:]
    rows = cells[0] * cells[1]
    area = jnp.transpose(master_area, (1, 0, 2))
    node_force, slave_force = pl.pallas_call(
        functools.partial(exchange_kernel, sizes),
        out_shape=(
            jax.ShapeDtypeStruct((3, rows, LANES), f32),
            jax.ShapeDtypeStruct((3, count, LANES), f32),
        ),
        in_specs=[HBM] * 11,
        out_specs=(VMEM,) * 2,
        scratch_shapes=[
            pltpu.VMEM(displacement.shape, f32),
            pltpu.VMEM(zone_mass.shape, f32),
            pltpu.VMEM(zone_energy.shape, f32),
            pltpu.VMEM((3, count, LANES), f32),
            pltpu.VMEM((count, LANES), f32),
            pltpu.VMEM((count, LANES), i32),
            pltpu.VMEM((1, count), i32),
            pltpu.VMEM((1, count), i32),
            pltpu.VMEM((masters, LANES), i32),
            pltpu.VMEM((3, masters, LANES), f32),
            pltpu.VMEM((masters, LANES), i32),
            pltpu.VMEM((peers, 1, LANES), f32),
            pltpu.VMEM((peers, 1, LANES), f32),
            pltpu.VMEM((sizes[2], masters, 4 * LANES), f32),
            pltpu.VMEM((peers, 32, LANES), f32),
            pltpu.VMEM((peers, 32, LANES), f32),
            pltpu.VMEM((peers, 8, LANES), f32),
            pltpu.VMEM((peers, 8, LANES), f32),
            pltpu.VMEM((sizes[2], masters, LANES), f32),
            pltpu.VMEM((sizes[2], masters, LANES), f32),
            pltpu.VMEM((peers, 32, LANES), f32),
            pltpu.VMEM((3, masters, LANES), f32),
            pltpu.VMEM((3 * LANES, 2 * rows), bf16),
            pltpu.VMEM((sizes[1], sizes[2], SLOTS, LANES), f32),
            pltpu.VMEM((sizes[2], masters, sizes[1] * SLOTS), bf16),
            pltpu.VMEM((peers, 32, LANES), f32),
            pltpu.VMEM((masters, LANES), f32),
            pltpu.VMEM((3, rows, LANES), f32),
            pltpu.VMEM((3 * LANES, rows), f32),
            pltpu.VMEM((5, cells[0] + 2, cells[1] + 8, LANES), f32),
            pltpu.VMEM((8, cells[0] + 8, LANES), f32),
            pltpu.VMEM((8, cells[0] + 8, LANES), f32),
            pltpu.VMEM((2, cells[1] + 8, LANES), f32),
            pltpu.VMEM((2, cells[1] + 8, LANES), f32),
            pltpu.SemaphoreType.DMA((11,)),
            pltpu.SemaphoreType.DMA((2, sizes[1])),
            pltpu.SemaphoreType.DMA((2, 2, sizes[2] // 2, 2)),
            pltpu.SemaphoreType.DMA((2, peers)),
            pltpu.SemaphoreType.DMA((2, peers)),
            pltpu.SemaphoreType.DMA((2, sizes[2])),
            pltpu.SemaphoreType.DMA((2, 8)),
        ],
        compiler_params=pltpu.CompilerParams(
            collective_id=0, has_side_effects=True, vmem_limit_bytes=63 * 2**20
        ),
        name="exchange",
    )(
        displacement,
        zone_mass,
        zone_energy,
        jnp.transpose(slave_position, (1, 0, 2)),
        slave_stiffness,
        slave_active,
        partner_peer.reshape(1, count),
        partner_block.reshape(1, count),
        master_node,
        area,
        face_active,
    )
    return (
        node_force.reshape((3,) + cells),
        jnp.transpose(slave_force, (1, 0, 2)),
    )


def solution(mesh):
    return jax.shard_map(
        body,
        mesh=mesh,
        in_specs=(
            P(None, "gx", "gy", "gz"),
            P("gx", "gy", "gz"),
            P("gx", "gy", "gz"),
            P(("gx", "gy", "gz"), None, None),
            P(("gx", "gy", "gz"), None),
            P(("gx", "gy", "gz"), None),
            P(("gx", "gy", "gz"), None),
            P(("gx", "gy", "gz"), None),
            P(("gx", "gy", "gz"), None),
            P(("gx", "gy", "gz"), None, None),
            P(("gx", "gy", "gz"), None),
        ),
        out_specs=(P(None, "gx", "gy", "gz"), P(("gx", "gy", "gz"), None, None)),
        check_vma=False,
    )
```
